32 devices in a mesh: batch: 8 (over y, x, core), head: 4 (over z).
Axes of the slice: x: 2, y: 2, z: 4, core: 2. Of those that a mesh axis runs over, the one named last changes fastest.
Arguments:
- tokens: bfloat16 [2, 3072, 2048], P(None, 'batch'), may hold values from -6 to 6
- cotangent: bfloat16 [2, 3072, 2048], P(None, 'batch'), may hold values from -6 to 6
- lengths: int32 [2, 8], P(None, 'batch'), may hold values from 48 to 384, as said below
- norm_in: float32 [2048], replicated, may hold values from 0.5 to 1.5
- w_query: bfloat16 [2048, 2048], P(None, 'head'), may hold values from -0.125 to 0.125
- w_key: bfloat16 [2048, 2048], P(None, 'head'), may hold values from -0.125 to 0.125
- w_value: bfloat16 [2048, 2048], P(None, 'head'), may hold values from -0.125 to 0.125
- w_gate: bfloat16 [2048, 2048], P(None, 'head'), may hold values from -0.125 to 0.125
- w_beta: bfloat16 [2048, 16], P(None, 'head'), may hold values from -0.125 to 0.125
- w_alpha: bfloat16 [2048, 16], P(None, 'head'), may hold values from -0.125 to 0.125
- conv_taps: float32 [3, 4, 2048], P(None, None, 'head'), may hold values from -2.5 to 2.5
- decay_log: float32 [16], P('head'), may hold values from -5 to -2.5
- decay_bias: float32 [16], P('head'), may hold values from -1 to 1
- norm_head: float32 [128], replicated, may hold values from 0.5 to 1.5
- w_out: bfloat16 [2048, 2048], P('head'), may hold values from -0.25 to 0.25
- norm_mid: float32 [2048], replicated, may hold values from 0.5 to 1.5
- w_up_gate: bfloat16 [2048, 5632], P(None, 'head'), may hold values from -0.125 to 0.125
- w_up: bfloat16 [2048, 5632], P(None, 'head'), may hold values from -0.125 to 0.125
- w_down: bfloat16 [5632, 2048], P('head'), may hold values from -0.109375 to 0.109375
Outputs:
- out_tokens: bfloat16 [2, 3072, 2048], P(None, 'batch')
- grad_tokens: bfloat16 [2, 3072, 2048], P(None, 'batch')
- grad_norm_in: float32 [2048], replicated
- grad_query: float32 [2048, 2048], P('batch', 'head')
- grad_key: float32 [2048, 2048], P('batch', 'head')
- grad_value: float32 [2048, 2048], P('batch', 'head')
- grad_gate: float32 [2048, 2048], P('batch', 'head')
- grad_beta: float32 [2048, 16], P('batch', 'head')
- grad_alpha: float32 [2048, 16], P('batch', 'head')
- grad_conv: float32 [3, 4, 2048], P(None, None, 'head')
- grad_decay_log: float32 [16], P('head')
- grad_decay_bias: float32 [16], P('head')
- grad_norm_head: float32 [128], replicated
- grad_out: float32 [2048, 2048], P('head', 'batch')
- grad_norm_mid: float32 [2048], replicated
- grad_up_gate: float32 [2048, 5632], P('batch', 'head')
- grad_up: float32 [2048, 5632], P('batch', 'head')
- grad_down: float32 [5632, 2048], P('head', 'batch')
The draws below stay inside these ranges and needn't reach their ends.
Inputs may be any that keep to these rules, and one draw needn't show every extreme that they name: `lengths`: in every micro-batch some slot's length is exactly 384.
All inputs are finite; a program needn't handle non-finite values.
Results may differ from the reference program's by a relative error of at most 0.017.
Values may be sent and summed in bfloat16 or wider, within the bound.
No kernel may reach another device: no remote copies, remote signals or barrier semaphores. Data moves between devices by JAX's collectives and lax.ppermute only.
A program may use at most 448 MiB of HBM per device.

```python
import math
import jax
import jax.numpy as jnp
from jax import lax

D = 2048
H = 16
DK = 128
FF = 5632
CONV = 4
BLOCK = 64
MICRO = 2
SLOT = 384
HD = 2048
TOKENS = 3072
N_BATCH = 8


def draw_lengths(key, part):
    key = jax.random.fold_in(key, 11)
    draw_key, second = jax.random.split(key)
    sampled = jax.random.randint(draw_key, (MICRO, N_BATCH), SLOT // 8, SLOT + 1)
    longest = jax.random.randint(second, (MICRO, 1), 0, N_BATCH)
    column = jnp.arange(N_BATCH, dtype=jnp.int32)[None, :]
    return jnp.where(column == longest, SLOT, sampled).astype(jnp.int32)


def shard_levels(rng, dims, cuts, low, largest):
    loudness = 1.0
    for position, parts in cuts:
        steps = jax.random.uniform(jax.random.fold_in(jax.random.fold_in(rng, 6), position), (parts,), jnp.float32, low / len(cuts), largest / len(cuts))
        loudness = loudness * jnp.repeat(jnp.exp(steps), dims[position] // parts).reshape((-1,) + (1,) * (len(dims) - 1 - position))
    return loudness


def scatter_about(stream_key, extent, deviation, bound, cuts=(), kind=jnp.bfloat16):
    entries = deviation * jax.random.normal(stream_key, extent, jnp.float32)
    if cuts:
        entries = entries * shard_levels(stream_key, extent, cuts, -0.22, 0.18)
    return jnp.clip(entries, -bound, bound).astype(kind)


def setup_inputs(seed: int = 0) -> dict:
    key_list = jax.random.split(jax.random.key(seed), 20)
    tokens = scatter_about(key_list[0], (MICRO, TOKENS, D), 1.0, 6.0, ((1, 8),))
    cotangent = scatter_about(key_list[1], (MICRO, TOKENS, D), 1.0, 6.0, ((1, 8),))
    lengths = draw_lengths(jax.random.fold_in(key_list[19], 71), 0)
    norm_in = jnp.clip(1.0 + 0.1 * jax.random.normal(key_list[3], (D,), jnp.float32), 0.5, 1.5)
    w_query = scatter_about(key_list[4], (D, HD), D ** -0.5, 0.125, ((1, 4),))
    w_key = scatter_about(key_list[5], (D, HD), D ** -0.5, 0.125, ((1, 4),))
    w_value = scatter_about(key_list[6], (D, HD), D ** -0.5, 0.125, ((1, 4),))
    w_gate = scatter_about(key_list[7], (D, HD), D ** -0.5, 0.125, ((1, 4),))
    w_beta = scatter_about(key_list[8], (D, H), D ** -0.5, 0.125, ((1, 4),))
    w_alpha = scatter_about(key_list[9], (D, H), D ** -0.5, 0.125, ((1, 4),))
    conv_taps = scatter_about(key_list[10], (3, CONV, HD), 0.5, 2.5, ((2, 4),), jnp.float32)
    decay_log = jnp.clip(-5.0 + 2.5 * jax.random.uniform(key_list[11], (H,), jnp.float32) ** shard_levels(key_list[11], (H,), ((0, 4),), -0.2, 0.2), -5.0, -2.5)
    decay_bias = jnp.clip(jax.random.uniform(key_list[12], (H,), jnp.float32, -1.0, 1.0) * shard_levels(key_list[12], (H,), ((0, 4),), -0.4, 0.0), -1.0, 1.0)
    norm_head = jnp.clip(1.0 + 0.1 * jax.random.normal(key_list[13], (DK,), jnp.float32), 0.5, 1.5)
    w_out = scatter_about(key_list[14], (HD, D), (HD // 4) ** -0.5, 0.25, ((0, 4),))
    norm_mid = jnp.clip(1.0 + 0.1 * jax.random.normal(key_list[15], (D,), jnp.float32), 0.5, 1.5)
    w_up_gate = scatter_about(key_list[16], (D, FF), D ** -0.5, 0.125, ((1, 4),))
    w_up = scatter_about(key_list[17], (D, FF), D ** -0.5, 0.125, ((1, 4),))
    w_down = scatter_about(key_list[18], (FF, D), (FF // 2) ** -0.5, 0.109375, ((0, 4),))
    return dict(tokens=tokens, cotangent=cotangent, lengths=lengths, norm_in=norm_in, w_query=w_query, w_key=w_key, w_value=w_value, w_gate=w_gate, w_beta=w_beta, w_alpha=w_alpha, conv_taps=conv_taps, decay_log=decay_log, decay_bias=decay_bias, norm_head=norm_head, w_out=w_out, norm_mid=norm_mid, w_up_gate=w_up_gate, w_up=w_up, w_down=w_down)


EPSILON = 1e-06
FULL_PRECISION = lax.Precision.HIGHEST

@jax.custom_vjp
def low(v):
    return lax.optimization_barrier(v.astype(jnp.bfloat16)).astype(jnp.float32)

@jax.custom_vjp
def low_back(v):
    return v

def low_keep(v):
    return (low(v), None)

def low_pass(kept, grad):
    return (grad,)

def back_keep(v):
    return (v, None)

def back_low(kept, grad):
    return (low(grad),)
low.defvjp(low_keep, low_pass)
low_back.defvjp(back_keep, back_low)

def exact_dot(left, right):
    return jnp.dot(left, right, precision=FULL_PRECISION)

def rms_scale(vector, gain):
    return vector * lax.rsqrt(lax.optimization_barrier(jnp.mean(vector * vector, axis=-1, keepdims=True)) + EPSILON) * gain

def unit_rows(vector):
    return vector * lax.rsqrt(lax.optimization_barrier(jnp.sum(vector * vector, axis=-1, keepdims=True)) + EPSILON)

def short_conv(projected, taps):
    tap_count = taps.shape[0]
    padded = jnp.concatenate([jnp.zeros((tap_count - 1, projected.shape[1]), jnp.float32), projected], axis=0)
    summed = jnp.zeros_like(projected)
    for offset in range(tap_count):
        summed = summed + padded[offset:offset + projected.shape[0]] * taps[offset]
    return summed

def delta_rule(queries, key_rows, values, beta_rows, decays):
    seq_len, head_count, head_dim = queries.shape
    blocks = seq_len // BLOCK

    def one_row(recurrent_state, pieces):
        current_query_row, current_key_row, current_value_row, beta_strength_row, decay_row = pieces
        recurrent_state = recurrent_state * jnp.exp(decay_row)[:, None, None]
        predicted_value = jnp.einsum('lix,li->lx', recurrent_state, current_key_row, precision=FULL_PRECISION)
        recurrent_state = recurrent_state + jnp.einsum('pz,ps->pzs', current_key_row, beta_strength_row[:, None] * (current_value_row - predicted_value), precision=FULL_PRECISION)
        output_vector = jnp.einsum('lix,li->lx', recurrent_state, current_query_row, precision=FULL_PRECISION)
        return (recurrent_state, output_vector)

    @jax.checkpoint
    def one_block(recurrent_state, pieces):
        return lax.scan(one_row, recurrent_state, pieces)

    def blocked(series):
        return series.reshape((blocks, BLOCK) + series.shape[1:])
    start_state = jnp.zeros((head_count, head_dim, head_dim), jnp.float32)
    last_state, outputs = lax.scan(one_block, start_state, (blocked(queries), blocked(key_rows), blocked(values), blocked(beta_rows), blocked(decays)))
    return outputs.reshape(seq_len, head_count, head_dim)

def mixer(projections, conv_taps, decay_log, decay_bias, norm_head):
    proj_query, proj_key, proj_value, proj_gate, proj_beta, proj_alpha = projections
    seq_len = proj_query.shape[0]
    split_shape = (seq_len, H, DK)
    queries = unit_rows(jax.nn.silu(short_conv(proj_query, conv_taps[0])).reshape(split_shape)) / math.sqrt(DK)
    key_rows = unit_rows(jax.nn.silu(short_conv(proj_key, conv_taps[1])).reshape(split_shape))
    values = jax.nn.silu(short_conv(proj_value, conv_taps[2])).reshape(split_shape)
    beta_rows = jax.nn.sigmoid(proj_beta)
    decays = -jnp.exp(decay_log) * jax.nn.softplus(proj_alpha + decay_bias)
    mixed_rows = delta_rule(queries, key_rows, values, beta_rows, decays)
    gated_rows = rms_scale(mixed_rows, norm_head) * jax.nn.silu(proj_gate.reshape(split_shape))
    return gated_rows.reshape(seq_len, H * DK)

def sequence_forward(rows, length, params):
    norm_in, w_query, w_key, w_value, w_gate, w_beta, w_alpha, conv_taps, decay_log, decay_bias, norm_head, w_out, norm_mid, w_up_gate, w_up, w_down = params
    keep = (jnp.arange(rows.shape[0], dtype=jnp.int32) < length.astype(jnp.int32)).astype(jnp.float32)[:, None]
    normed = low(rms_scale(rows, norm_in))
    projections = tuple((low_back(exact_dot(normed, weight)) for weight in (w_query, w_key, w_value, w_gate, w_beta, w_alpha)))
    gated_rows = low(mixer(projections, conv_taps, decay_log, decay_bias, norm_head))
    middle = rows + keep * low_back(exact_dot(gated_rows, w_out))
    mid_normed = low(rms_scale(middle, norm_mid))
    gate_act = low_back(exact_dot(mid_normed, w_up_gate))
    up_act = low_back(exact_dot(mid_normed, w_up))
    hidden = low(jax.nn.silu(gate_act) * up_act)
    return middle + keep * low_back(exact_dot(hidden, w_down))

def reference(tokens, cotangent, lengths, norm_in, w_query, w_key, w_value, w_gate, w_beta, w_alpha, conv_taps, decay_log, decay_bias, norm_head, w_out, norm_mid, w_up_gate, w_up, w_down):
    params = tuple((argument.astype(jnp.float32) for argument in (norm_in, w_query, w_key, w_value, w_gate, w_beta, w_alpha, conv_taps, decay_log, decay_bias, norm_head, w_out, norm_mid, w_up_gate, w_up, w_down)))
    seq_count = MICRO * N_BATCH
    flat_rows = tokens.astype(jnp.float32).reshape(seq_count, SLOT, D)
    flat_lengths = lengths.reshape(seq_count).astype(jnp.int32)
    checked = jax.checkpoint(sequence_forward)

    def forward(all_rows, weights):

        def one_sequence(counter, pieces):
            return (counter, checked(pieces[0], pieces[1], weights))
        unused, results = lax.scan(one_sequence, jnp.zeros((), jnp.float32), (all_rows, flat_lengths))
        return results
    results, pullback = jax.vjp(forward, flat_rows, params)
    grad_rows, grad_params = pullback(cotangent.astype(jnp.float32).reshape(seq_count, SLOT, D))
    grad_norm_in, grad_query, grad_key, grad_value, grad_gate, grad_beta, grad_alpha, grad_conv, grad_decay_log, grad_decay_bias, grad_norm_head, grad_out, grad_norm_mid, grad_up_gate, grad_up, grad_down = grad_params
    out_tokens = results.reshape(MICRO, TOKENS, D).astype(jnp.bfloat16)
    grad_tokens = grad_rows.reshape(MICRO, TOKENS, D).astype(jnp.bfloat16)
    return (out_tokens, grad_tokens, grad_norm_in, grad_query, grad_key, grad_value, grad_gate, grad_beta, grad_alpha, grad_conv, grad_decay_log, grad_decay_bias, grad_norm_head, grad_out, grad_norm_mid, grad_up_gate, grad_up, grad_down)
```

```python
import math

import jax
import jax.numpy as jnp
from jax import lax
from jax.experimental import pallas as pl
from jax.experimental.pallas import tpu as pltpu
from jax.sharding import PartitionSpec as P

EPSILON = 1e-06
CHUNK = 128
LOW = jnp.bfloat16
FULL = jnp.float32


def mm(left, right, dims=((1,), (0,))):
    return lax.dot_general(
        left.astype(LOW), right.astype(LOW), (dims, ((), ())), preferred_element_type=FULL
    )


NN = ((1,), (0,))
NT = ((1,), (1,))
TN = ((0,), (0,))


def mm3(left, right, dims):
    left_high = left.astype(LOW)
    left_rest = (left - left_high.astype(FULL)).astype(LOW)
    right_high = right.astype(LOW)
    right_rest = (right - right_high.astype(FULL)).astype(LOW)
    return (
        mm(left_high, right_high, dims)
        + mm(left_high, right_rest, dims)
        + mm(left_rest, right_high, dims)
    )


def row_sum(value):
    return jnp.sum(value, axis=-1, keepdims=True)


def shift_down(value, count):
    if count == 0:
        return value
    row = lax.broadcasted_iota(jnp.int32, value.shape, 0)
    return jnp.where(row >= count, pltpu.roll(value, count, 0), 0.0)


def shift_up(value, count):
    if count == 0:
        return value
    rows = value.shape[0]
    row = lax.broadcasted_iota(jnp.int32, value.shape, 0)
    return jnp.where(row < rows - count, pltpu.roll(value, rows - count, 0), 0.0)


def conv_rows(projected, taps):
    count = taps.shape[0]
    total = projected * taps[count - 1 : count]
    for tap in range(count - 1):
        total = total + shift_down(projected, count - 1 - tap) * taps[tap : tap + 1]
    return total


def conv_back(grad, projected, taps):
    count = taps.shape[0]
    grad_in = grad * taps[count - 1 : count]
    grad_taps = [None] * count
    grad_taps[count - 1] = jnp.sum(grad * projected, axis=0, keepdims=True)
    for tap in range(count - 1):
        grad_in = grad_in + shift_up(grad, count - 1 - tap) * taps[tap : tap + 1]
        grad_taps[tap] = jnp.sum(
            grad * shift_down(projected, count - 1 - tap), axis=0, keepdims=True
        )
    return grad_in, grad_taps


def column_of(matrix, index):
    lane = lax.broadcasted_iota(jnp.int32, matrix.shape, 1)
    return row_sum(jnp.where(lane == index, matrix, 0.0))


def chunk_parts(rows):
    return [slice(start, start + CHUNK) for start in range(0, rows, CHUNK)]


def masks():
    row = lax.broadcasted_iota(jnp.int32, (CHUNK, CHUNK), 0)
    col = lax.broadcasted_iota(jnp.int32, (CHUNK, CHUNK), 1)
    return row, col


def sigmoid(value):
    return 1.0 / (1.0 + jnp.exp(-value))


def softplus(value):
    return jnp.maximum(value, 0.0) + jnp.log1p(jnp.exp(-jnp.abs(value)))


def full_dot(left, right):
    return lax.dot_general(
        left,
        right,
        (((1,), (0,)), ((), ())),
        precision=lax.Precision.HIGHEST,
        preferred_element_type=FULL,
    )


def decay_tables(alpha_ref, beta_ref, dlog_ref, dbias_ref, first_head, head_count, parts):
    row, col = masks()
    lower = jnp.where(row >= col, 1.0, 0.0)
    shifted = alpha_ref[...] + dbias_ref[...]
    decays = -jnp.exp(dlog_ref[...]) * softplus(shifted)
    running = [full_dot(lower, decays[part]) for part in parts]
    betas = sigmoid(beta_ref[...])
    tables = []
    for head in range(head_count):
        beta_col = column_of(betas, first_head + head)
        per_chunk = []
        for index, part in enumerate(parts):
            gamma = column_of(running[index], first_head + head)
            spread = jnp.broadcast_to(gamma, (CHUNK, CHUNK))
            spread = spread - spread.T
            causal = jnp.where(row >= col, jnp.exp(jnp.where(row >= col, spread, 0.0)), 0.0)
            last = gamma[CHUNK - 1 : CHUNK]
            per_chunk.append(
                (beta_col[part], jnp.exp(gamma), jnp.exp(last - gamma), jnp.exp(last), causal)
            )
        tables.append(per_chunk)
    return decays, betas, shifted, tables


def unit_inverse(value):
    return lax.rsqrt(row_sum(value * value) + EPSILON)


def mixer_forward_body(
    query_ref, key_ref, value_ref, gate_ref, beta_ref, alpha_ref, taps_ref, dlog_ref, dbias_ref,
    gain_ref, gated_ref, mixed_ref, fresh_ref, inverse_ref, state_ref,
):
    rows, width = query_ref.shape
    head_dim = gain_ref.shape[1]
    head_count = width // head_dim
    parts = chunk_parts(rows)
    first_head = pl.program_id(0) * head_count
    row, col = masks()
    tables = decay_tables(
        alpha_ref, beta_ref, dlog_ref, dbias_ref, first_head, head_count, parts
    )[3]
    units = [(head, index) for head in range(head_count) for index in range(len(parts))]
    queries, key_rows, values = {}, {}, {}
    for head in range(head_count):
        cols = slice(head * head_dim, (head + 1) * head_dim)
        conv_q = conv_rows(query_ref[:, cols], taps_ref[0, :, cols])
        conv_k = conv_rows(key_ref[:, cols], taps_ref[1, :, cols])
        conv_v = conv_rows(value_ref[:, cols], taps_ref[2, :, cols])
        act_q = conv_q * sigmoid(conv_q)
        act_k = conv_k * sigmoid(conv_k)
        query = (act_q * (unit_inverse(act_q) * (1.0 / math.sqrt(head_dim)))).astype(LOW)
        key_low = (act_k * unit_inverse(act_k)).astype(LOW)
        value = conv_v * sigmoid(conv_v)
        for index, part in enumerate(parts):
            queries[head, index] = query[part]
            key_rows[head, index] = key_low[part]
            values[head, index] = value[part]
    system, scores, inverse = {}, {}, {}
    for head, index in units:
        beta, _, _, _, causal = tables[head][index]
        key_blk = key_rows[head, index]
        system[head, index] = jnp.where(row > col, beta * mm(key_blk, key_blk, NT) * causal, 0.0)
        scores[head, index] = (mm(queries[head, index], key_blk, NT) * causal).astype(LOW)
    size = 1
    while size < CHUNK:
        own = (row // (2 * size) == col // (2 * size)) & (row // size != col // size)
        for unit in units:
            part = jnp.where(own, system[unit], 0.0)
            if size == 1:
                inverse[unit] = jnp.where(row == col, 1.0, 0.0) - part
            else:
                inverse_low = inverse[unit].astype(LOW)
                inverse[unit] = inverse[unit] - mm(mm(inverse_low, part), inverse_low)
        size *= 2
    gain = gain_ref[...]
    states = {head: jnp.zeros((head_dim, head_dim), FULL) for head in range(head_count)}
    for index, part in enumerate(parts):
        for head in range(head_count):
            unit = (head, index)
            cols = slice(head * head_dim, (head + 1) * head_dim)
            beta, start, tail, last, _ = tables[head][index]
            state = states[head]
            state_ref[head, index] = state.astype(LOW)
            inverse_low = inverse[unit].astype(LOW)
            inverse_ref[head, index] = inverse_low
            right = values[unit]
            if index:
                right = right - start * mm(key_rows[unit], state)
            fresh = mm(inverse_low, beta * right)
            fresh_low = fresh.astype(LOW)
            fresh_ref[part, cols] = fresh_low
            mixed = mm(scores[unit], fresh_low)
            if index:
                mixed = mixed + start * mm(queries[unit], state)
            mixed_ref[part, cols] = mixed
            if index + 1 < len(parts):
                grown = mm(key_rows[unit].astype(FULL) * tail, fresh_low, TN)
                states[head] = last * state + grown if index else grown
            gate = gate_ref[part, cols]
            scale = lax.rsqrt(jnp.mean(mixed * mixed, axis=-1, keepdims=True) + EPSILON)
            gated_ref[part, cols] = (mixed * scale * gain * (gate * sigmoid(gate))).astype(LOW)


def mixer_backward_body(
    grad_ref, query_ref, key_ref, value_ref, gate_ref, beta_ref, alpha_ref, taps_ref, dlog_ref,
    dbias_ref, gain_ref, mixed_ref, fresh_ref, inverse_ref, state_ref,
    dquery_ref, dkey_ref, dvalue_ref, dgate_ref, dbeta_ref, dalpha_ref, dtaps_ref, ddlog_ref,
    ddbias_ref, dgain_ref,
):
    rows, width = query_ref.shape
    head_dim = gain_ref.shape[1]
    head_count = width // head_dim
    parts = chunk_parts(rows)
    step = pl.program_id(0)
    first_head = step * head_count
    row, col = masks()
    decays, betas, shifted, tables = decay_tables(
        alpha_ref, beta_ref, dlog_ref, dbias_ref, first_head, head_count, parts
    )
    upper = jnp.where(row <= col, 1.0, 0.0)
    units = [(head, index) for head in range(head_count) for index in range(len(parts))]
    gain = gain_ref[...]
    root = 1.0 / math.sqrt(head_dim)

    @pl.when(step == 0)
    def _():
        dbeta_ref[...] = jnp.zeros_like(dbeta_ref)
        dalpha_ref[...] = jnp.zeros_like(dalpha_ref)
        ddlog_ref[...] = jnp.zeros_like(ddlog_ref)
        ddbias_ref[...] = jnp.zeros_like(ddbias_ref)
        dgain_ref[...] = jnp.zeros_like(dgain_ref)

    queries, key_rows, values, grads, acts, convs = {}, {}, {}, {}, {}, {}
    for head in range(head_count):
        cols = slice(head * head_dim, (head + 1) * head_dim)
        conv_q = conv_rows(query_ref[:, cols], taps_ref[0, :, cols])
        conv_k = conv_rows(key_ref[:, cols], taps_ref[1, :, cols])
        conv_v = conv_rows(value_ref[:, cols], taps_ref[2, :, cols])
        act_q = conv_q * sigmoid(conv_q)
        act_k = conv_k * sigmoid(conv_k)
        value = conv_v * sigmoid(conv_v)
        norm_q, norm_k = unit_inverse(act_q), unit_inverse(act_k)
        query, key_full = act_q * norm_q, act_k * norm_k
        convs[head] = (conv_q, conv_k, conv_v)
        acts[head] = (query, norm_q, key_full, norm_k)
        mixed = mixed_ref[:, cols]
        gate = gate_ref[:, cols]
        sig = sigmoid(gate)
        grad = grad_ref[:, cols]
        scale = lax.rsqrt(jnp.mean(mixed * mixed, axis=-1, keepdims=True) + EPSILON)
        normal = mixed * scale
        opened = gate * sig
        dgain_ref[...] += jnp.sum(grad * normal * opened, axis=0, keepdims=True)
        dgate_ref[:, cols] = (
            grad * normal * gain * (sig * (1.0 + gate * (1.0 - sig)))
        ).astype(LOW)
        grad_normal = grad * gain * opened
        grad_mixed = scale * (
            grad_normal - normal * jnp.mean(grad_normal * normal, axis=-1, keepdims=True)
        )
        for index, part in enumerate(parts):
            queries[head, index] = query[part] * root
            key_rows[head, index] = key_full[part]
            values[head, index] = value[part]
            grads[head, index] = grad_mixed[part]
    cross, scores, system, strict = {}, {}, {}, {}
    for unit in units:
        head, index = unit
        beta, _, _, _, causal = tables[head][index]
        cross[unit] = mm3(queries[unit], key_rows[unit], NT)
        scores[unit] = (cross[unit] * causal).astype(LOW)
        strict[unit] = jnp.where(row > col, beta * causal, 0.0)
        system[unit] = mm3(key_rows[unit], key_rows[unit], NT)
    grad_states = {head: None for head in range(head_count)}
    grad_q, grad_k, grad_v, gamma_grads = {}, {}, {}, {}
    grad_beta = {}
    for index in reversed(range(len(parts))):
        part = parts[index]
        for head in range(head_count):
            unit = (head, index)
            cols = slice(head * head_dim, (head + 1) * head_dim)
            beta, start, tail, last, causal = tables[head][index]
            query, key_full = queries[unit], key_rows[unit]
            query_low, key_low = query.astype(LOW), key_full.astype(LOW)
            grad = grads[unit]
            grad_low = grad.astype(LOW)
            fresh_low = fresh_ref[part, cols]
            fresh = fresh_low.astype(FULL)
            state = state_ref[head, index]
            grad_state = grad_states[head]
            grad_fresh = mm(scores[unit], grad_low, TN)
            if grad_state is not None:
                grad_state_low = grad_state.astype(LOW)
                grad_fresh = grad_fresh + mm(key_full * tail, grad_state_low)
            grad_right = mm(inverse_ref[head, index], grad_fresh, TN)
            grad_right_low = grad_right.astype(LOW)
            grad_cross = mm(grad_low, fresh_low, NT) * causal
            grad_system = -(mm(grad_right_low, fresh_low, NT) * strict[unit])
            turned = grad_cross * cross[unit] + grad_system * system[unit]
            gamma = row_sum(turned) - row_sum(turned.T)
            grad_cross_low = grad_cross.astype(LOW)
            grad_system_low = grad_system.astype(LOW)
            dquery = mm(grad_cross_low, key_low)
            dkey = (
                mm(grad_system_low, key_low)
                + mm(grad_system_low, key_low, TN)
                + mm(grad_cross_low, query_low, TN)
            )
            back = -beta * start * grad_right
            if index:
                back_low = back.astype(LOW)
                dquery = dquery + start * mm(grad_low, state, NT)
                dkey = dkey + mm(back_low, state, NT)
                gamma = gamma + row_sum(grad * start * mm(query_low, state))
                gamma = gamma + row_sum(back * mm(key_low, state))
            final = None
            if grad_state is not None:
                grad_tail = mm(fresh_low, grad_state_low, NT) * tail
                dkey = dkey + grad_tail
                tail_term = row_sum(grad_tail * key_full)
                gamma = gamma - tail_term
                final = jnp.sum(tail_term, axis=0, keepdims=True)
                if index:
                    final = final + last * jnp.sum(
                        row_sum(state.astype(FULL) * grad_state), axis=0, keepdims=True
                    )
                is_last = lax.broadcasted_iota(jnp.int32, gamma.shape, 0) == CHUNK - 1
                gamma = gamma + jnp.where(is_last, final, 0.0)
            gamma_grads[unit] = gamma
            grad_beta[unit] = (1.0 - beta) * row_sum(grad_right * fresh)
            grad_q[unit], grad_k[unit], grad_v[unit] = dquery, dkey, beta * grad_right
            if index:
                grown = mm(query * start, grad_low, TN) + mm(key_low, back_low, TN)
                if grad_state is not None:
                    grown = grown + last * grad_state
                grad_states[head] = grown
    lane = lax.broadcasted_iota(jnp.int32, (CHUNK, alpha_ref.shape[1]), 1)
    for index, part in enumerate(parts):
        gamma_cols = jnp.zeros(lane.shape, FULL)
        beta_cols = jnp.zeros(lane.shape, FULL)
        for head in range(head_count):
            gamma_cols = jnp.where(lane == first_head + head, gamma_grads[head, index], gamma_cols)
            beta_cols = jnp.where(lane == first_head + head, grad_beta[head, index], beta_cols)
        grad_decay = full_dot(upper, gamma_cols)
        grad_alpha = grad_decay * -jnp.exp(dlog_ref[...]) * sigmoid(shifted[part])
        dbeta_ref[part] += beta_cols
        dalpha_ref[part] += grad_alpha
        ddbias_ref[...] += jnp.sum(grad_alpha, axis=0, keepdims=True)
        ddlog_ref[...] += jnp.sum(grad_decay * decays[part], axis=0, keepdims=True)
    for head in range(head_count):
        cols = slice(head * head_dim, (head + 1) * head_dim)
        query, norm_q, key_full, norm_k = acts[head]
        dquery = jnp.concatenate([grad_q[head, index] for index in range(len(parts))], axis=0)
        dkey = jnp.concatenate([grad_k[head, index] for index in range(len(parts))], axis=0)
        dvalue = jnp.concatenate([grad_v[head, index] for index in range(len(parts))], axis=0)
        act_grads = (
            norm_q * root * (dquery - query * row_sum(query * dquery)),
            norm_k * (dkey - key_full * row_sum(key_full * dkey)),
            dvalue,
        )
        projected = (query_ref, key_ref, value_ref)
        for which, out_ref in enumerate((dquery_ref, dkey_ref, dvalue_ref)):
            conv = convs[head][which]
            sig = sigmoid(conv)
            grad_conv = act_grads[which] * sig * (1.0 + conv * (1.0 - sig))
            grad_in, grad_taps = conv_back(
                grad_conv, projected[which][:, cols], taps_ref[which, :, cols]
            )
            out_ref[:, cols] = grad_in.astype(LOW)
            for tap, entry in enumerate(grad_taps):
                dtaps_ref[which, tap : tap + 1, cols] = entry


def mixer_specs(rows, heads, group, head_dim, taps_shape):
    width = group * head_dim
    wide = pl.BlockSpec((rows, width), lambda step: (0, step))
    narrow = pl.BlockSpec((rows, heads), lambda step: (0, 0))
    taps = pl.BlockSpec(taps_shape[:2] + (width,), lambda step: (0, 0, step))
    small = pl.BlockSpec((1, heads), lambda step: (0, 0))
    gain = pl.BlockSpec((1, head_dim), lambda step: (0, 0))
    chunks = rows // CHUNK
    square = pl.BlockSpec((group, chunks, CHUNK, CHUNK), lambda step: (step, 0, 0, 0))
    state = pl.BlockSpec((group, chunks, head_dim, head_dim), lambda step: (step, 0, 0, 0))
    return wide, narrow, taps, small, gain, square, state


def mixer_forward(projections, conv_taps, decay_log, decay_bias, norm_head):
    query, key_rows, value, gate, beta, alpha = projections
    rows, width = query.shape
    heads, head_dim = decay_log.shape[0], norm_head.shape[0]
    group = 2 if heads % 2 == 0 else 1
    chunks = rows // CHUNK
    wide, narrow, taps, small, gain, square, state = mixer_specs(
        rows, heads, group, head_dim, conv_taps.shape
    )
    return pl.pallas_call(
        mixer_forward_body,
        grid=(heads // group,),
        in_specs=[wide] * 4 + [narrow] * 2 + [taps, small, small, gain],
        out_specs=[wide, wide, wide, square, state],
        out_shape=[
            jax.ShapeDtypeStruct((rows, width), LOW),
            jax.ShapeDtypeStruct((rows, width), FULL),
            jax.ShapeDtypeStruct((rows, width), LOW),
            jax.ShapeDtypeStruct((heads, chunks, CHUNK, CHUNK), LOW),
            jax.ShapeDtypeStruct((heads, chunks, head_dim, head_dim), LOW),
        ],
        compiler_params=pltpu.CompilerParams(
            vmem_limit_bytes=48 * 1024 * 1024, dimension_semantics=("arbitrary",)
        ),
        name="mixer_forward",
    )(
        query, key_rows, value, gate, beta, alpha, conv_taps,
        decay_log.reshape(1, heads), decay_bias.reshape(1, heads), norm_head.reshape(1, head_dim),
    )


def mixer_backward(grad, projections, conv_taps, decay_log, decay_bias, norm_head, kept):
    query, key_rows, value, gate, beta, alpha = projections
    mixed, fresh, inverse, states = kept
    rows, width = query.shape
    heads, head_dim = decay_log.shape[0], norm_head.shape[0]
    group = 2 if heads % 2 == 0 else 1
    wide, narrow, taps, small, gain, square, state = mixer_specs(
        rows, heads, group, head_dim, conv_taps.shape
    )
    return pl.pallas_call(
        mixer_backward_body,
        grid=(heads // group,),
        in_specs=[wide] * 5
        + [narrow] * 2
        + [taps, small, small, gain, wide, wide, square, state],
        out_specs=[wide] * 4 + [narrow] * 2 + [taps, small, small, gain],
        out_shape=[jax.ShapeDtypeStruct((rows, width), LOW)] * 4
        + [jax.ShapeDtypeStruct((rows, heads), FULL)] * 2
        + [
            jax.ShapeDtypeStruct(conv_taps.shape, FULL),
            jax.ShapeDtypeStruct((1, heads), FULL),
            jax.ShapeDtypeStruct((1, heads), FULL),
            jax.ShapeDtypeStruct((1, head_dim), FULL),
        ],
        compiler_params=pltpu.CompilerParams(
            vmem_limit_bytes=48 * 1024 * 1024, dimension_semantics=("arbitrary",)
        ),
        name="mixer_backward",
    )(
        grad, query, key_rows, value, gate, beta, alpha, conv_taps,
        decay_log.reshape(1, heads), decay_bias.reshape(1, heads), norm_head.reshape(1, head_dim),
        mixed, fresh, inverse, states,
    )


def rms_scale(vector, gain):
    return vector * lax.rsqrt(jnp.mean(vector * vector, axis=-1, keepdims=True) + EPSILON) * gain


def rms_back(grad_norm, vector, gain):
    inverse = lax.rsqrt(jnp.mean(vector * vector, axis=-1, keepdims=True) + EPSILON)
    normal = vector * inverse
    scaled = grad_norm * gain
    return inverse * (scaled - normal * jnp.mean(scaled * normal, axis=-1, keepdims=True))


def scatter_sum(partial_sum):
    return lax.psum_scatter(
        partial_sum.astype(LOW), "head", scatter_dimension=0, tiled=True
    ).astype(FULL)


def gather(own):
    return lax.all_gather(own, "head", axis=0, tiled=True)


def per_device(
    tokens, cotangent, lengths, norm_in, w_query, w_key, w_value, w_gate, w_beta, w_alpha,
    conv_taps, decay_log, decay_bias, norm_head, w_out, norm_mid, w_up_gate, w_up, w_down,
):
    micro_count, seq_len, model_dim = tokens.shape
    head_parts = lax.axis_size("head")
    batch_parts = lax.axis_size("batch")
    own_len = seq_len // head_parts
    first_row = lax.axis_index("head") * own_len
    positions = lax.broadcasted_iota(jnp.int32, (seq_len, 1), 0)
    in_weights = (w_query, w_key, w_value, w_gate, w_beta, w_alpha)

    def own_of(value):
        return lax.dynamic_slice_in_dim(value, first_row, own_len, 0)

    micros = []
    for micro in range(micro_count):
        rows = tokens[micro].astype(FULL)
        keep = (positions < lengths[micro, 0]).astype(FULL)
        normed = rms_scale(rows, norm_in).astype(LOW)
        projections = tuple(mm(normed, weight) for weight in in_weights)
        gated, *kept = mixer_forward(projections, conv_taps, decay_log, decay_bias, norm_head)
        out_part = scatter_sum(mm(gated, w_out))
        micros.append(
            dict(rows=own_of(rows), keep=keep, keep_own=own_of(keep), normed=normed,
                 projections=projections, gated=gated, kept=kept, out_part=out_part)
        )
    for micro in range(micro_count):
        held = micros[micro]
        middle = held["rows"] + held["keep_own"] * held["out_part"]
        mid = gather(rms_scale(middle, norm_mid).astype(LOW))
        grad_rows = cotangent[micro].astype(FULL)
        down_grad = (held["keep"] * grad_rows).astype(LOW)
        gate_act = mm(mid, w_up_gate)
        up_act = mm(mid, w_up)
        sig = jax.nn.sigmoid(gate_act)
        hidden = (gate_act * sig * up_act).astype(LOW)
        grad_hidden = mm(down_grad, w_down, NT)
        grad_gate = (grad_hidden * up_act * sig * (1.0 + gate_act * (1.0 - sig))).astype(LOW)
        grad_up = (grad_hidden * gate_act * sig).astype(LOW)
        mid_part = scatter_sum(mm(grad_gate, w_up_gate, NT) + mm(grad_up, w_up, NT))
        down_part = scatter_sum(mm(hidden, w_down))
        out_own = (middle + held["keep_own"] * down_part).astype(LOW)
        held.update(
            middle=middle, mid=mid, down_grad=down_grad, hidden=hidden, grad_gate=grad_gate,
            grad_up=grad_up, mid_part=mid_part, grad_rows=own_of(grad_rows), out=gather(out_own),
        )

    def both(name):
        return jnp.concatenate([held[name] for held in micros], axis=0)

    def shared(left, right):
        return lax.psum_scatter(
            mm(left, right, TN).astype(LOW), "batch", scatter_dimension=0, tiled=True
        ).astype(FULL)

    mid_both, down_both = both("mid"), both("down_grad")
    share_up_gate = shared(mid_both, both("grad_gate"))
    share_up = shared(mid_both, both("grad_up"))
    share_down = shared(down_both, both("hidden")).T
    gain_in = jnp.zeros((model_dim,), FULL)
    gain_mid = jnp.zeros((model_dim,), FULL)
    small = None
    for micro in range(micro_count):
        held = micros[micro]
        middle = held["middle"]
        gain_mid = gain_mid + jnp.sum(rms_scale(middle, 1.0) * held["mid_part"], axis=0)
        grad_middle = held["grad_rows"] + rms_back(held["mid_part"], middle, norm_mid)
        attn = gather((held["keep_own"] * grad_middle).astype(LOW))
        *grads, grad_taps, grad_dlog, grad_dbias, grad_gain = mixer_backward(
            mm(attn, w_out, NT), held["projections"], conv_taps, decay_log, decay_bias,
            norm_head, held["kept"],
        )
        grads = [entry.astype(LOW) for entry in grads]
        in_part = mm(grads[0], in_weights[0], NT)
        for index in range(1, len(in_weights)):
            in_part = in_part + mm(grads[index], in_weights[index], NT)
        in_part = scatter_sum(in_part)
        gain_in = gain_in + jnp.sum(rms_scale(held["rows"], 1.0) * in_part, axis=0)
        grad_own = (grad_middle + rms_back(in_part, held["rows"], norm_in)).astype(LOW)
        entries = (grad_taps, grad_dlog, grad_dbias, grad_gain)
        small = entries if small is None else tuple(a + b for a, b in zip(small, entries))
        held.update(attn=attn, grads=grads, grad_tokens=gather(grad_own))
    normed_both = both("normed")
    grads_both = [
        jnp.concatenate([held["grads"][index] for held in micros], axis=0) for index in range(6)
    ]
    share_in = [shared(normed_both, grads_both[index]) for index in range(4)]
    share_out = shared(both("attn"), both("gated")).T
    tiny = mm(jnp.concatenate(grads_both[4:], axis=1), normed_both, TN)
    grad_taps, grad_dlog, grad_dbias, grad_gain = small
    gains = lax.psum((gain_in, grad_gain[0], gain_mid), ("batch", "head"))
    tiny, grad_taps, grad_dlog, grad_dbias = lax.psum(
        (tiny, grad_taps, grad_dlog[0], grad_dbias[0]), "batch"
    )
    width = model_dim // batch_parts
    tiny = lax.dynamic_slice_in_dim(tiny, lax.axis_index("batch") * width, width, 1).T
    count = w_beta.shape[1]
    return (
        jnp.stack([held["out"] for held in micros]),
        jnp.stack([held["grad_tokens"] for held in micros]),
        gains[0],
        share_in[0], share_in[1], share_in[2], share_in[3],
        tiny[:, :count], tiny[:, count:],
        grad_taps, grad_dlog, grad_dbias, gains[1],
        share_out, gains[2], share_up_gate, share_up, share_down,
    )


def solution(mesh):
    tokens, column, row = P(None, "batch", None), P(None, "head"), P("head", None)
    placed = (
        tokens, tokens, P(None, "batch"), P(), column, column, column, column, column, column,
        P(None, None, "head"), P("head"), P("head"), P(), row, P(), column, column, row,
    )
    block, turned = P("batch", "head"), P("head", "batch")
    return jax.shard_map(
        per_device,
        mesh=mesh,
        in_specs=placed,
        out_specs=(
            tokens, tokens, P(), block, block, block, block, block, block,
            P(None, None, "head"), P("head"), P("head"), P(), turned, P(), block, block, turned,
        ),
        check_vma=False,
    )
```

```python
import math

import jax
import jax.numpy as jnp
from jax import lax
from jax.experimental import pallas as pl
from jax.experimental.pallas import tpu as pltpu
from jax.sharding import PartitionSpec as P

EPSILON = 1e-06
CHUNK = 128
LOW = jnp.bfloat16
FULL = jnp.float32


def mm(left, right, dims=((1,), (0,))):
    return lax.dot_general(
        left.astype(LOW), right.astype(LOW), (dims, ((), ())), preferred_element_type=FULL
    )


NN = ((1,), (0,))
NT = ((1,), (1,))
TN = ((0,), (0,))


def mm3(left, right, dims):
    left_high = left.astype(LOW)
    left_rest = (left - left_high.astype(FULL)).astype(LOW)
    right_high = right.astype(LOW)
    right_rest = (right - right_high.astype(FULL)).astype(LOW)
    return (
        mm(left_high, right_high, dims)
        + mm(left_high, right_rest, dims)
        + mm(left_rest, right_high, dims)
    )


def row_sum(value):
    return jnp.sum(value, axis=-1, keepdims=True)


def shift_down(value, count):
    if count == 0:
        return value
    row = lax.broadcasted_iota(jnp.int32, value.shape, 0)
    return jnp.where(row >= count, pltpu.roll(value, count, 0), 0.0)


def shift_up(value, count):
    if count == 0:
        return value
    rows = value.shape[0]
    row = lax.broadcasted_iota(jnp.int32, value.shape, 0)
    return jnp.where(row < rows - count, pltpu.roll(value, rows - count, 0), 0.0)


def conv_rows(projected, taps):
    count = taps.shape[0]
    total = projected * taps[count - 1 : count]
    for tap in range(count - 1):
        total = total + shift_down(projected, count - 1 - tap) * taps[tap : tap + 1]
    return total


def conv_back(grad, projected, taps):
    count = taps.shape[0]
    grad_in = grad * taps[count - 1 : count]
    grad_taps = [None] * count
    grad_taps[count - 1] = jnp.sum(grad * projected, axis=0, keepdims=True)
    for tap in range(count - 1):
        grad_in = grad_in + shift_up(grad, count - 1 - tap) * taps[tap : tap + 1]
        grad_taps[tap] = jnp.sum(
            grad * shift_down(projected, count - 1 - tap), axis=0, keepdims=True
        )
    return grad_in, grad_taps


def column_of(matrix, index):
    lane = lax.broadcasted_iota(jnp.int32, matrix.shape, 1)
    return row_sum(jnp.where(lane == index, matrix, 0.0))


def chunk_parts(rows):
    return [slice(start, start + CHUNK) for start in range(0, rows, CHUNK)]


def masks():
    row = lax.broadcasted_iota(jnp.int32, (CHUNK, CHUNK), 0)
    col = lax.broadcasted_iota(jnp.int32, (CHUNK, CHUNK), 1)
    return row, col


def sigmoid(value):
    return 1.0 / (1.0 + jnp.exp(-value))


def softplus(value):
    return jnp.maximum(value, 0.0) + jnp.log1p(jnp.exp(-jnp.abs(value)))


def full_dot(left, right):
    return lax.dot_general(
        left,
        right,
        (((1,), (0,)), ((), ())),
        precision=lax.Precision.HIGHEST,
        preferred_element_type=FULL,
    )


def decay_tables(alpha_ref, beta_ref, dlog_ref, dbias_ref, first_head, head_count, parts):
    row, col = masks()
    lower = jnp.where(row >= col, 1.0, 0.0)
    shifted = alpha_ref[...] + dbias_ref[...]
    decays = -jnp.exp(dlog_ref[...]) * softplus(shifted)
    running = [full_dot(lower, decays[part]) for part in parts]
    betas = sigmoid(beta_ref[...])
    tables = []
    for head in range(head_count):
        beta_col = column_of(betas, first_head + head)
        per_chunk = []
        for index, part in enumerate(parts):
            gamma = column_of(running[index], first_head + head)
            spread = jnp.broadcast_to(gamma, (CHUNK, CHUNK))
            spread = spread - spread.T
            causal = jnp.where(row >= col, jnp.exp(jnp.where(row >= col, spread, 0.0)), 0.0)
            last = gamma[CHUNK - 1 : CHUNK]
            per_chunk.append(
                (beta_col[part], jnp.exp(gamma), jnp.exp(last - gamma), jnp.exp(last), causal)
            )
        tables.append(per_chunk)
    return decays, betas, shifted, tables


def unit_inverse(value):
    return lax.rsqrt(row_sum(value * value) + EPSILON)


def mixer_forward_body(
    query_ref, key_ref, value_ref, gate_ref, beta_ref, alpha_ref, taps_ref, dlog_ref, dbias_ref,
    gain_ref, gated_ref, mixed_ref, fresh_ref, inverse_ref, state_ref,
):
    rows, width = query_ref.shape
    head_dim = gain_ref.shape[1]
    head_count = width // head_dim
    parts = chunk_parts(rows)
    first_head = pl.program_id(0) * head_count
    row, col = masks()
    tables = decay_tables(
        alpha_ref, beta_ref, dlog_ref, dbias_ref, first_head, head_count, parts
    )[3]
    units = [(head, index) for head in range(head_count) for index in range(len(parts))]
    queries, key_rows, values = {}, {}, {}
    for head in range(head_count):
        cols = slice(head * head_dim, (head + 1) * head_dim)
        conv_q = conv_rows(query_ref[:, cols], taps_ref[0, :, cols])
        conv_k = conv_rows(key_ref[:, cols], taps_ref[1, :, cols])
        conv_v = conv_rows(value_ref[:, cols], taps_ref[2, :, cols])
        act_q = conv_q * sigmoid(conv_q)
        act_k = conv_k * sigmoid(conv_k)
        query = (act_q * (unit_inverse(act_q) * (1.0 / math.sqrt(head_dim)))).astype(LOW)
        key_low = (act_k * unit_inverse(act_k)).astype(LOW)
        value = conv_v * sigmoid(conv_v)
        for index, part in enumerate(parts):
            queries[head, index] = query[part]
            key_rows[head, index] = key_low[part]
            values[head, index] = value[part]
    system, scores, inverse = {}, {}, {}
    for head, index in units:
        beta, _, _, _, causal = tables[head][index]
        key_blk = key_rows[head, index]
        system[head, index] = jnp.where(row > col, beta * mm(key_blk, key_blk, NT) * causal, 0.0)
        scores[head, index] = (mm(queries[head, index], key_blk, NT) * causal).astype(LOW)
    size = 1
    while size < CHUNK:
        own = (row // (2 * size) == col // (2 * size)) & (row // size != col // size)
        for unit in units:
            part = jnp.where(own, system[unit], 0.0)
            if size == 1:
                inverse[unit] = jnp.where(row == col, 1.0, 0.0) - part
            else:
                inverse_low = inverse[unit].astype(LOW)
                inverse[unit] = inverse[unit] - mm(mm(inverse_low, part), inverse_low)
        size *= 2
    gain = gain_ref[...]
    states = {head: jnp.zeros((head_dim, head_dim), FULL) for head in range(head_count)}
    for index, part in enumerate(parts):
        for head in range(head_count):
            unit = (head, index)
            cols = slice(head * head_dim, (head + 1) * head_dim)
            beta, start, tail, last, _ = tables[head][index]
            state = states[head]
            state_ref[head, index] = state.astype(LOW)
            inverse_low = inverse[unit].astype(LOW)
            inverse_ref[head, index] = inverse_low
            right = values[unit]
            if index:
                right = right - start * mm(key_rows[unit], state)
            fresh = mm(inverse_low, beta * right)
            fresh_low = fresh.astype(LOW)
            fresh_ref[part, cols] = fresh_low
            mixed = mm(scores[unit], fresh_low)
            if index:
                mixed = mixed + start * mm(queries[unit], state)
            mixed_ref[part, cols] = mixed
            if index + 1 < len(parts):
                grown = mm(key_rows[unit].astype(FULL) * tail, fresh_low, TN)
                states[head] = last * state + grown if index else grown
            gate = gate_ref[part, cols]
            scale = lax.rsqrt(jnp.mean(mixed * mixed, axis=-1, keepdims=True) + EPSILON)
            gated_ref[part, cols] = (mixed * scale * gain * (gate * sigmoid(gate))).astype(LOW)


def mixer_backward_body(
    grad_ref, query_ref, key_ref, value_ref, gate_ref, beta_ref, alpha_ref, taps_ref, dlog_ref,
    dbias_ref, gain_ref, mixed_ref, fresh_ref, inverse_ref, state_ref,
    dproj_ref, dbeta_ref, dalpha_ref, dtaps_ref, ddlog_ref, ddbias_ref, dgain_ref,
):
    rows, width = query_ref.shape
    head_dim = gain_ref.shape[1]
    head_count = width // head_dim
    parts = chunk_parts(rows)
    step = pl.program_id(0)
    first_head = step * head_count
    row, col = masks()
    decays, betas, shifted, tables = decay_tables(
        alpha_ref, beta_ref, dlog_ref, dbias_ref, first_head, head_count, parts
    )
    upper = jnp.where(row <= col, 1.0, 0.0)
    units = [(head, index) for head in range(head_count) for index in range(len(parts))]
    gain = gain_ref[...]
    root = 1.0 / math.sqrt(head_dim)
    all_cols = dproj_ref.shape[1] // 4

    def proj_cols(which, head):
        start = which * all_cols + (first_head + head) * head_dim
        return pl.ds(pl.multiple_of(start, head_dim), head_dim)

    @pl.when(step == 0)
    def _():
        dbeta_ref[...] = jnp.zeros_like(dbeta_ref)
        dalpha_ref[...] = jnp.zeros_like(dalpha_ref)
        ddlog_ref[...] = jnp.zeros_like(ddlog_ref)
        ddbias_ref[...] = jnp.zeros_like(ddbias_ref)
        dgain_ref[...] = jnp.zeros_like(dgain_ref)

    queries, key_rows, values, grads, acts, convs = {}, {}, {}, {}, {}, {}
    for head in range(head_count):
        cols = slice(head * head_dim, (head + 1) * head_dim)
        conv_q = conv_rows(query_ref[:, cols], taps_ref[0, :, cols])
        conv_k = conv_rows(key_ref[:, cols], taps_ref[1, :, cols])
        conv_v = conv_rows(value_ref[:, cols], taps_ref[2, :, cols])
        act_q = conv_q * sigmoid(conv_q)
        act_k = conv_k * sigmoid(conv_k)
        value = conv_v * sigmoid(conv_v)
        norm_q, norm_k = unit_inverse(act_q), unit_inverse(act_k)
        query, key_full = act_q * norm_q, act_k * norm_k
        convs[head] = (conv_q, conv_k, conv_v)
        acts[head] = (query, norm_q, key_full, norm_k)
        mixed = mixed_ref[:, cols]
        gate = gate_ref[:, cols]
        sig = sigmoid(gate)
        grad = grad_ref[:, cols]
        scale = lax.rsqrt(jnp.mean(mixed * mixed, axis=-1, keepdims=True) + EPSILON)
        normal = mixed * scale
        opened = gate * sig
        dgain_ref[...] += jnp.sum(grad * normal * opened, axis=0, keepdims=True)
        dproj_ref[:, proj_cols(3, head)] = (
            grad * normal * gain * (sig * (1.0 + gate * (1.0 - sig)))
        ).astype(LOW)
        grad_normal = grad * gain * opened
        grad_mixed = scale * (
            grad_normal - normal * jnp.mean(grad_normal * normal, axis=-1, keepdims=True)
        )
        for index, part in enumerate(parts):
            queries[head, index] = query[part] * root
            key_rows[head, index] = key_full[part]
            values[head, index] = value[part]
            grads[head, index] = grad_mixed[part]
    cross, scores, system, strict = {}, {}, {}, {}
    for unit in units:
        head, index = unit
        beta, _, _, _, causal = tables[head][index]
        cross[unit] = mm3(queries[unit], key_rows[unit], NT)
        scores[unit] = (cross[unit] * causal).astype(LOW)
        strict[unit] = jnp.where(row > col, beta * causal, 0.0)
        system[unit] = mm3(key_rows[unit], key_rows[unit], NT)
    grad_states = {head: None for head in range(head_count)}
    grad_q, grad_k, grad_v, gamma_grads = {}, {}, {}, {}
    grad_beta = {}
    for index in reversed(range(len(parts))):
        part = parts[index]
        for head in range(head_count):
            unit = (head, index)
            cols = slice(head * head_dim, (head + 1) * head_dim)
            beta, start, tail, last, causal = tables[head][index]
            query, key_full = queries[unit], key_rows[unit]
            query_low, key_low = query.astype(LOW), key_full.astype(LOW)
            grad = grads[unit]
            grad_low = grad.astype(LOW)
            fresh_low = fresh_ref[part, cols]
            fresh = fresh_low.astype(FULL)
            state = state_ref[head, index]
            grad_state = grad_states[head]
            grad_fresh = mm(scores[unit], grad_low, TN)
            if grad_state is not None:
                grad_state_low = grad_state.astype(LOW)
                grad_fresh = grad_fresh + mm(key_full * tail, grad_state_low)
            grad_right = mm(inverse_ref[head, index], grad_fresh, TN)
            grad_right_low = grad_right.astype(LOW)
            grad_cross = mm(grad_low, fresh_low, NT) * causal
            grad_system = -(mm(grad_right_low, fresh_low, NT) * strict[unit])
            turned = grad_cross * cross[unit] + grad_system * system[unit]
            gamma = row_sum(turned) - row_sum(turned.T)
            grad_cross_low = grad_cross.astype(LOW)
            grad_system_low = grad_system.astype(LOW)
            dquery = mm(grad_cross_low, key_low)
            dkey = (
                mm(grad_system_low, key_low)
                + mm(grad_system_low, key_low, TN)
                + mm(grad_cross_low, query_low, TN)
            )
            back = -beta * start * grad_right
            if index:
                back_low = back.astype(LOW)
                dquery = dquery + start * mm(grad_low, state, NT)
                dkey = dkey + mm(back_low, state, NT)
                gamma = gamma + row_sum(grad * start * mm(query_low, state))
                gamma = gamma + row_sum(back * mm(key_low, state))
            final = None
            if grad_state is not None:
                grad_tail = mm(fresh_low, grad_state_low, NT) * tail
                dkey = dkey + grad_tail
                tail_term = row_sum(grad_tail * key_full)
                gamma = gamma - tail_term
                final = jnp.sum(tail_term, axis=0, keepdims=True)
                if index:
                    final = final + last * jnp.sum(
                        row_sum(state.astype(FULL) * grad_state), axis=0, keepdims=True
                    )
                is_last = lax.broadcasted_iota(jnp.int32, gamma.shape, 0) == CHUNK - 1
                gamma = gamma + jnp.where(is_last, final, 0.0)
            gamma_grads[unit] = gamma
            grad_beta[unit] = (1.0 - beta) * row_sum(grad_right * fresh)
            grad_q[unit], grad_k[unit], grad_v[unit] = dquery, dkey, beta * grad_right
            if index:
                grown = mm(query * start, grad_low, TN) + mm(key_low, back_low, TN)
                if grad_state is not None:
                    grown = grown + last * grad_state
                grad_states[head] = grown
    lane = lax.broadcasted_iota(jnp.int32, (CHUNK, alpha_ref.shape[1]), 1)
    for index, part in enumerate(parts):
        gamma_cols = jnp.zeros(lane.shape, FULL)
        beta_cols = jnp.zeros(lane.shape, FULL)
        for head in range(head_count):
            gamma_cols = jnp.where(lane == first_head + head, gamma_grads[head, index], gamma_cols)
            beta_cols = jnp.where(lane == first_head + head, grad_beta[head, index], beta_cols)
        grad_decay = full_dot(upper, gamma_cols)
        grad_alpha = grad_decay * -jnp.exp(dlog_ref[...]) * sigmoid(shifted[part])
        dbeta_ref[part] += beta_cols
        dalpha_ref[part] += grad_alpha
        ddbias_ref[...] += jnp.sum(grad_alpha, axis=0, keepdims=True)
        ddlog_ref[...] += jnp.sum(grad_decay * decays[part], axis=0, keepdims=True)
    for head in range(head_count):
        cols = slice(head * head_dim, (head + 1) * head_dim)
        query, norm_q, key_full, norm_k = acts[head]
        dquery = jnp.concatenate([grad_q[head, index] for index in range(len(parts))], axis=0)
        dkey = jnp.concatenate([grad_k[head, index] for index in range(len(parts))], axis=0)
        dvalue = jnp.concatenate([grad_v[head, index] for index in range(len(parts))], axis=0)
        act_grads = (
            norm_q * root * (dquery - query * row_sum(query * dquery)),
            norm_k * (dkey - key_full * row_sum(key_full * dkey)),
            dvalue,
        )
        projected = (query_ref, key_ref, value_ref)
        for which in range(3):
            conv = convs[head][which]
            sig = sigmoid(conv)
            grad_conv = act_grads[which] * sig * (1.0 + conv * (1.0 - sig))
            grad_in, grad_taps = conv_back(
                grad_conv, projected[which][:, cols], taps_ref[which, :, cols]
            )
            dproj_ref[:, proj_cols(which, head)] = grad_in.astype(LOW)
            for tap, entry in enumerate(grad_taps):
                dtaps_ref[which, tap : tap + 1, cols] = entry


def mixer_specs(rows, heads, group, head_dim, taps_shape):
    width = group * head_dim
    wide = pl.BlockSpec((rows, width), lambda step: (0, step))
    narrow = pl.BlockSpec((rows, heads), lambda step: (0, 0))
    taps = pl.BlockSpec(taps_shape[:2] + (width,), lambda step: (0, 0, step))
    small = pl.BlockSpec((1, heads), lambda step: (0, 0))
    gain = pl.BlockSpec((1, head_dim), lambda step: (0, 0))
    chunks = rows // CHUNK
    square = pl.BlockSpec((group, chunks, CHUNK, CHUNK), lambda step: (step, 0, 0, 0))
    state = pl.BlockSpec((group, chunks, head_dim, head_dim), lambda step: (step, 0, 0, 0))
    return wide, narrow, taps, small, gain, square, state


def mixer_forward(projections, conv_taps, decay_log, decay_bias, norm_head):
    query, key_rows, value, gate, beta, alpha = projections
    rows, width = query.shape
    heads, head_dim = decay_log.shape[0], norm_head.shape[0]
    group = 2 if heads % 2 == 0 else 1
    chunks = rows // CHUNK
    wide, narrow, taps, small, gain, square, state = mixer_specs(
        rows, heads, group, head_dim, conv_taps.shape
    )
    return pl.pallas_call(
        mixer_forward_body,
        grid=(heads // group,),
        in_specs=[wide] * 4 + [narrow] * 2 + [taps, small, small, gain],
        out_specs=[wide, wide, wide, square, state],
        out_shape=[
            jax.ShapeDtypeStruct((rows, width), LOW),
            jax.ShapeDtypeStruct((rows, width), FULL),
            jax.ShapeDtypeStruct((rows, width), LOW),
            jax.ShapeDtypeStruct((heads, chunks, CHUNK, CHUNK), LOW),
            jax.ShapeDtypeStruct((heads, chunks, head_dim, head_dim), LOW),
        ],
        compiler_params=pltpu.CompilerParams(
            vmem_limit_bytes=48 * 1024 * 1024, dimension_semantics=("arbitrary",)
        ),
        name="mixer_forward",
    )(
        query, key_rows, value, gate, beta, alpha, conv_taps,
        decay_log.reshape(1, heads), decay_bias.reshape(1, heads), norm_head.reshape(1, head_dim),
    )


def mixer_backward(grad, projections, conv_taps, decay_log, decay_bias, norm_head, kept):
    query, key_rows, value, gate, beta, alpha = projections
    mixed, fresh, inverse, states = kept
    rows, width = query.shape
    heads, head_dim = decay_log.shape[0], norm_head.shape[0]
    group = 2 if heads % 2 == 0 else 1
    wide, narrow, taps, small, gain, square, state = mixer_specs(
        rows, heads, group, head_dim, conv_taps.shape
    )
    return pl.pallas_call(
        mixer_backward_body,
        grid=(heads // group,),
        in_specs=[wide] * 5
        + [narrow] * 2
        + [taps, small, small, gain, wide, wide, square, state],
        out_specs=[pl.BlockSpec((rows, 4 * width), lambda step: (0, 0))]
        + [narrow] * 2
        + [taps, small, small, gain],
        out_shape=[jax.ShapeDtypeStruct((rows, 4 * width), LOW)]
        + [jax.ShapeDtypeStruct((rows, heads), FULL)] * 2
        + [
            jax.ShapeDtypeStruct(conv_taps.shape, FULL),
            jax.ShapeDtypeStruct((1, heads), FULL),
            jax.ShapeDtypeStruct((1, heads), FULL),
            jax.ShapeDtypeStruct((1, head_dim), FULL),
        ],
        compiler_params=pltpu.CompilerParams(
            vmem_limit_bytes=48 * 1024 * 1024, dimension_semantics=("arbitrary",)
        ),
        name="mixer_backward",
    )(
        grad, query, key_rows, value, gate, beta, alpha, conv_taps,
        decay_log.reshape(1, heads), decay_bias.reshape(1, heads), norm_head.reshape(1, head_dim),
        mixed, fresh, inverse, states,
    )


def rms_scale(vector, gain):
    return vector * lax.rsqrt(jnp.mean(vector * vector, axis=-1, keepdims=True) + EPSILON) * gain


def rms_back(grad_norm, vector, gain):
    inverse = lax.rsqrt(jnp.mean(vector * vector, axis=-1, keepdims=True) + EPSILON)
    normal = vector * inverse
    scaled = grad_norm * gain
    return inverse * (scaled - normal * jnp.mean(scaled * normal, axis=-1, keepdims=True))


def chain_scatter(partial_sum):
    parts = lax.axis_size("head")
    place = lax.axis_index("head")
    own_len = partial_sum.shape[0] // parts

    def share(index):
        start = jnp.clip(index, 0, parts - 1) * own_len
        return lax.dynamic_slice_in_dim(partial_sum, start, own_len, 0).astype(FULL)

    right = left = 0.0
    for step in range(1, parts):
        right = lax.ppermute(
            (share(parts - step + place) + right).astype(LOW),
            "head",
            [(source, source + 1) for source in range(step)],
        ).astype(FULL)
        left = lax.ppermute(
            (share(step - parts + place) + left).astype(LOW),
            "head",
            [(source, source - 1) for source in range(parts - step, parts)],
        ).astype(FULL)
    return share(place) + right + left


def chain_gather(own):
    parts = lax.axis_size("head")
    place = lax.axis_index("head")
    own_len = own.shape[0]
    right = left = own
    before, after = [], []
    for step in range(1, parts):
        right = lax.ppermute(
            right, "head", [(source, source + 1) for source in range(step - 1, parts - 1)]
        )
        left = lax.ppermute(
            left, "head", [(source, source - 1) for source in range(1, parts - step + 1)]
        )
        before.append(right)
        after.append(left)
    joined = jnp.concatenate(before[::-1] + [own] + after, axis=0)
    return lax.dynamic_slice_in_dim(
        joined, (parts - 1 - place) * own_len, parts * own_len, 0
    )


def offload_scatter(partial_sum):
    return lax.psum_scatter(
        partial_sum.astype(LOW), "head", scatter_dimension=0, tiled=True
    ).astype(FULL)


def offload_gather(own):
    return lax.all_gather(own, "head", axis=0, tiled=True)


def butterfly(value, axis):
    size = lax.axis_size(axis)
    bit = 1
    while bit < size:
        value = value + lax.ppermute(value, axis, [(place, place ^ bit) for place in range(size)])
        bit *= 2
    return value


def packed(entries):
    flat = jnp.concatenate([entry.reshape(-1) for entry in entries])
    pad = -flat.shape[0] % 1024
    return jnp.pad(flat, (0, pad)).reshape(-1, 128)


def unpacked(matrix, entries):
    flat = matrix.reshape(-1)
    outs, start = [], 0
    for entry in entries:
        outs.append(flat[start : start + entry.size].reshape(entry.shape))
        start += entry.size
    return outs


def after(value, *others):
    return lax.optimization_barrier((value,) + others)[0]


scatter_out, gather_mid = chain_scatter, chain_gather
scatter_down, gather_out = offload_scatter, offload_gather
scatter_mid, gather_attn = chain_scatter, chain_gather
scatter_in, gather_in = chain_scatter, chain_gather


def per_device(
    tokens, cotangent, lengths, norm_in, w_query, w_key, w_value, w_gate, w_beta, w_alpha,
    conv_taps, decay_log, decay_bias, norm_head, w_out, norm_mid, w_up_gate, w_up, w_down,
):
    micro_count, seq_len, model_dim = tokens.shape
    head_parts = lax.axis_size("head")
    batch_parts = lax.axis_size("batch")
    own_len = seq_len // head_parts
    first_row = lax.axis_index("head") * own_len
    positions = lax.broadcasted_iota(jnp.int32, (seq_len, 1), 0)
    in_weights = (w_query, w_key, w_value, w_gate)
    hidden_width = w_up.shape[1]
    head_width = w_query.shape[1]

    def own_of(value):
        return lax.dynamic_slice_in_dim(value, first_row, own_len, 0)

    micros = []
    for micro in range(micro_count):
        rows = tokens[micro].astype(FULL)
        grad_rows = cotangent[micro].astype(FULL)
        keep = (positions < lengths[micro, 0]).astype(FULL)
        normed = rms_scale(rows, norm_in).astype(LOW)
        projections = tuple(mm(normed, weight) for weight in in_weights + (w_beta, w_alpha))
        gated, *kept = mixer_forward(projections, conv_taps, decay_log, decay_bias, norm_head)
        out_part = scatter_out(mm(gated, w_out).astype(LOW))
        micros.append(
            dict(rows=own_of(rows), grad_rows=own_of(grad_rows), keep_own=own_of(keep),
                 down_grad=(keep * grad_rows).astype(LOW), normed=normed,
                 projections=projections, gated=gated, kept=kept, out_part=out_part)
        )
    for held in micros:
        middle = held["rows"] + held["keep_own"] * held["out_part"]
        mid = gather_mid(rms_scale(middle, norm_mid).astype(LOW))
        gate_act = mm(mid, w_up_gate)
        up_act = mm(mid, w_up)
        sig = jax.nn.sigmoid(gate_act)
        hidden = (gate_act * sig * up_act).astype(LOW)
        grad_hidden = mm(held["down_grad"], w_down, NT)
        grad_gate = (grad_hidden * up_act * sig * (1.0 + gate_act * (1.0 - sig))).astype(LOW)
        grad_up = (grad_hidden * gate_act * sig).astype(LOW)
        mid_part = scatter_mid((mm(grad_gate, w_up_gate, NT) + mm(grad_up, w_up, NT)).astype(LOW))
        down_part = scatter_down(mm(hidden, w_down).astype(LOW))
        out_own = (middle + held["keep_own"] * down_part).astype(LOW)
        held.update(
            middle=middle, mid=mid, hidden=hidden, grad_gate=grad_gate, grad_up=grad_up,
            mid_part=mid_part, out=gather_out(out_own),
        )

    def both(*names):
        return jnp.concatenate(
            [jnp.concatenate([held[name] for name in names], axis=1) for held in micros], axis=0
        )

    def shared(left, right):
        return lax.psum_scatter(
            mm(left, right, TN).astype(LOW), "batch", scatter_dimension=0, tiled=True
        ).astype(FULL)

    share_ups = shared(both("mid"), both("grad_gate", "grad_up"))
    share_down = shared(both("down_grad"), both("hidden")).T
    gain_in = jnp.zeros((model_dim,), FULL)
    gain_mid = jnp.zeros((model_dim,), FULL)
    small = None
    for held in micros:
        middle = held["middle"]
        gain_mid = gain_mid + jnp.sum(rms_scale(middle, 1.0) * held["mid_part"], axis=0)
        grad_middle = held["grad_rows"] + rms_back(held["mid_part"], middle, norm_mid)
        attn = gather_attn((held["keep_own"] * grad_middle).astype(LOW))
        grads, grad_beta, grad_alpha, grad_taps, grad_dlog, grad_dbias, grad_gain = mixer_backward(
            mm(attn, w_out, NT), held["projections"], conv_taps, decay_log, decay_bias,
            norm_head, held["kept"],
        )
        narrow = (grad_beta.astype(LOW), grad_alpha.astype(LOW))
        in_part = mm(narrow[0], w_beta, NT) + mm(narrow[1], w_alpha, NT)
        for index, weight in enumerate(in_weights):
            in_part = in_part + mm(
                grads[:, index * head_width : (index + 1) * head_width], weight, NT
            )
        in_part = scatter_in(in_part.astype(LOW))
        gain_in = gain_in + jnp.sum(rms_scale(held["rows"], 1.0) * in_part, axis=0)
        grad_own = (grad_middle + rms_back(in_part, held["rows"], norm_in)).astype(LOW)
        entries = (grad_taps, grad_dlog, grad_dbias, grad_gain)
        small = entries if small is None else tuple(a + b for a, b in zip(small, entries))
        held.update(attn=attn, grads=grads, beta=narrow[0], alpha=narrow[1],
                    grad_tokens=gather_in(grad_own))
    share_out = shared(both("attn"), both("gated")).T
    normed_both = both("normed")
    share_in = shared(normed_both, both("grads"))
    tiny = mm(both("beta", "alpha"), normed_both, TN)
    grad_taps, grad_dlog, grad_dbias, grad_gain = small
    entries = (tiny, grad_taps, grad_dlog[0], grad_dbias[0])
    tiny, grad_taps, grad_dlog, grad_dbias = unpacked(
        butterfly(packed(entries), "batch"), entries
    )
    entries = (gain_in, grad_gain[0], gain_mid)
    gains = unpacked(butterfly(butterfly(packed(entries), "batch"), "head"), entries)
    width = model_dim // batch_parts
    tiny = lax.dynamic_slice_in_dim(tiny, lax.axis_index("batch") * width, width, 1).T
    count = w_beta.shape[1]
    return (
        jnp.stack([held["out"] for held in micros]),
        jnp.stack([held["grad_tokens"] for held in micros]),
        gains[0],
        *(share_in[:, index * head_width : (index + 1) * head_width] for index in range(4)),
        tiny[:, :count], tiny[:, count:],
        grad_taps, grad_dlog, grad_dbias, gains[1],
        share_out, gains[2], share_ups[:, :hidden_width], share_ups[:, hidden_width:], share_down,
    )


def solution(mesh):
    tokens, column, row = P(None, "batch", None), P(None, "head"), P("head", None)
    placed = (
        tokens, tokens, P(None, "batch"), P(), column, column, column, column, column, column,
        P(None, None, "head"), P("head"), P("head"), P(), row, P(), column, column, row,
    )
    block, turned = P("batch", "head"), P("head", "batch")
    return jax.shard_map(
        per_device,
        mesh=mesh,
        in_specs=placed,
        out_specs=(
            tokens, tokens, P(), block, block, block, block, block, block,
            P(None, None, "head"), P("head"), P("head"), P(), turned, P(), block, block, turned,
        ),
        check_vma=False,
    )
```

```python
import math

import jax
import jax.numpy as jnp
from jax import lax
from jax.experimental import pallas as pl
from jax.experimental.pallas import tpu as pltpu
from jax.sharding import PartitionSpec as P

EPSILON = 1e-06
CHUNK = 128
LOW = jnp.bfloat16
FULL = jnp.float32


def mm(left, right, dims=((1,), (0,))):
    return lax.dot_general(
        left.astype(LOW), right.astype(LOW), (dims, ((), ())), preferred_element_type=FULL
    )


NN = ((1,), (0,))
NT = ((1,), (1,))
TN = ((0,), (0,))


def mm3(left, right, dims):
    left_high = left.astype(LOW)
    left_rest = (left - left_high.astype(FULL)).astype(LOW)
    right_high = right.astype(LOW)
    right_rest = (right - right_high.astype(FULL)).astype(LOW)
    return (
        mm(left_high, right_high, dims)
        + mm(left_high, right_rest, dims)
        + mm(left_rest, right_high, dims)
    )


def row_sum(value):
    return jnp.sum(value, axis=-1, keepdims=True)


def shift_down(value, count):
    if count == 0:
        return value
    row = lax.broadcasted_iota(jnp.int32, value.shape, 0)
    return jnp.where(row >= count, pltpu.roll(value, count, 0), 0.0)


def shift_up(value, count):
    if count == 0:
        return value
    rows = value.shape[0]
    row = lax.broadcasted_iota(jnp.int32, value.shape, 0)
    return jnp.where(row < rows - count, pltpu.roll(value, rows - count, 0), 0.0)


def conv_rows(projected, taps):
    count = taps.shape[0]
    total = projected * taps[count - 1 : count]
    for tap in range(count - 1):
        total = total + shift_down(projected, count - 1 - tap) * taps[tap : tap + 1]
    return total


def conv_back(grad, projected, taps):
    count = taps.shape[0]
    grad_in = grad * taps[count - 1 : count]
    grad_taps = [None] * count
    grad_taps[count - 1] = jnp.sum(grad * projected, axis=0, keepdims=True)
    for tap in range(count - 1):
        grad_in = grad_in + shift_up(grad, count - 1 - tap) * taps[tap : tap + 1]
        grad_taps[tap] = jnp.sum(
            grad * shift_down(projected, count - 1 - tap), axis=0, keepdims=True
        )
    return grad_in, grad_taps


def column_of(matrix, index):
    lane = lax.broadcasted_iota(jnp.int32, matrix.shape, 1)
    return row_sum(jnp.where(lane == index, matrix, 0.0))


def chunk_parts(rows):
    return [slice(start, start + CHUNK) for start in range(0, rows, CHUNK)]


def masks():
    row = lax.broadcasted_iota(jnp.int32, (CHUNK, CHUNK), 0)
    col = lax.broadcasted_iota(jnp.int32, (CHUNK, CHUNK), 1)
    return row, col


def sigmoid(value):
    return 1.0 / (1.0 + jnp.exp(-value))


def softplus(value):
    return jnp.maximum(value, 0.0) + jnp.log1p(jnp.exp(-jnp.abs(value)))


def full_dot(left, right):
    return lax.dot_general(
        left,
        right,
        (((1,), (0,)), ((), ())),
        precision=lax.Precision.HIGHEST,
        preferred_element_type=FULL,
    )


def decay_tables(alpha_ref, beta_ref, dlog_ref, dbias_ref, first_head, head_count, parts):
    row, col = masks()
    lower = jnp.where(row >= col, 1.0, 0.0)
    shifted = alpha_ref[...] + dbias_ref[...]
    decays = -jnp.exp(dlog_ref[...]) * softplus(shifted)
    running = [full_dot(lower, decays[part]) for part in parts]
    betas = sigmoid(beta_ref[...])
    tables = []
    for head in range(head_count):
        beta_col = column_of(betas, first_head + head)
        per_chunk = []
        for index, part in enumerate(parts):
            gamma = column_of(running[index], first_head + head)
            spread = jnp.broadcast_to(gamma, (CHUNK, CHUNK))
            spread = spread - spread.T
            causal = jnp.where(row >= col, jnp.exp(jnp.where(row >= col, spread, 0.0)), 0.0)
            last = gamma[CHUNK - 1 : CHUNK]
            per_chunk.append(
                (beta_col[part], jnp.exp(gamma), jnp.exp(last - gamma), jnp.exp(last), causal)
            )
        tables.append(per_chunk)
    return decays, betas, shifted, tables


def unit_inverse(value):
    return lax.rsqrt(row_sum(value * value) + EPSILON)


def mixer_forward_body(
    query_ref, key_ref, value_ref, gate_ref, beta_ref, alpha_ref, taps_ref, dlog_ref, dbias_ref,
    gain_ref, gated_ref, mixed_ref, fresh_ref, inverse_ref, state_ref,
):
    rows, width = query_ref.shape
    head_dim = gain_ref.shape[1]
    head_count = width // head_dim
    parts = chunk_parts(rows)
    first_head = pl.program_id(0) * head_count
    row, col = masks()
    tables = decay_tables(
        alpha_ref, beta_ref, dlog_ref, dbias_ref, first_head, head_count, parts
    )[3]
    units = [(head, index) for head in range(head_count) for index in range(len(parts))]
    queries, key_rows, values = {}, {}, {}
    for head in range(head_count):
        cols = slice(head * head_dim, (head + 1) * head_dim)
        conv_q = conv_rows(query_ref[:, cols], taps_ref[0, :, cols])
        conv_k = conv_rows(key_ref[:, cols], taps_ref[1, :, cols])
        conv_v = conv_rows(value_ref[:, cols], taps_ref[2, :, cols])
        act_q = conv_q * sigmoid(conv_q)
        act_k = conv_k * sigmoid(conv_k)
        query = (act_q * (unit_inverse(act_q) * (1.0 / math.sqrt(head_dim)))).astype(LOW)
        key_low = (act_k * unit_inverse(act_k)).astype(LOW)
        value = conv_v * sigmoid(conv_v)
        for index, part in enumerate(parts):
            queries[head, index] = query[part]
            key_rows[head, index] = key_low[part]
            values[head, index] = value[part]
    system, scores, inverse = {}, {}, {}
    for head, index in units:
        beta, _, _, _, causal = tables[head][index]
        key_blk = key_rows[head, index]
        system[head, index] = jnp.where(row > col, beta * mm(key_blk, key_blk, NT) * causal, 0.0)
        scores[head, index] = (mm(queries[head, index], key_blk, NT) * causal).astype(LOW)
    size = 1
    while size < CHUNK:
        own = (row // (2 * size) == col // (2 * size)) & (row // size != col // size)
        for unit in units:
            part = jnp.where(own, system[unit], 0.0)
            if size == 1:
                inverse[unit] = jnp.where(row == col, 1.0, 0.0) - part
            else:
                inverse_low = inverse[unit].astype(LOW)
                inverse[unit] = inverse[unit] - mm(mm(inverse_low, part), inverse_low)
        size *= 2
    gain = gain_ref[...]
    states = {head: jnp.zeros((head_dim, head_dim), FULL) for head in range(head_count)}
    for index, part in enumerate(parts):
        for head in range(head_count):
            unit = (head, index)
            cols = slice(head * head_dim, (head + 1) * head_dim)
            beta, start, tail, last, _ = tables[head][index]
            state = states[head]
            state_ref[head, index] = state.astype(LOW)
            inverse_low = inverse[unit].astype(LOW)
            inverse_ref[head, index] = inverse_low
            right = values[unit]
            if index:
                right = right - start * mm(key_rows[unit], state)
            fresh = mm(inverse_low, beta * right)
            fresh_low = fresh.astype(LOW)
            fresh_ref[part, cols] = fresh_low
            mixed = mm(scores[unit], fresh_low)
            if index:
                mixed = mixed + start * mm(queries[unit], state)
            mixed_ref[part, cols] = mixed
            if index + 1 < len(parts):
                grown = mm(key_rows[unit].astype(FULL) * tail, fresh_low, TN)
                states[head] = last * state + grown if index else grown
            gate = gate_ref[part, cols]
            scale = lax.rsqrt(jnp.mean(mixed * mixed, axis=-1, keepdims=True) + EPSILON)
            gated_ref[part, cols] = (mixed * scale * gain * (gate * sigmoid(gate))).astype(LOW)


def mixer_backward_body(
    grad_ref, query_ref, key_ref, value_ref, gate_ref, beta_ref, alpha_ref, taps_ref, dlog_ref,
    dbias_ref, gain_ref, mixed_ref, fresh_ref, inverse_ref, state_ref,
    dproj_ref, dbeta_ref, dalpha_ref, dtaps_ref, ddlog_ref, ddbias_ref, dgain_ref,
):
    rows, width = query_ref.shape
    head_dim = gain_ref.shape[1]
    head_count = width // head_dim
    parts = chunk_parts(rows)
    step = pl.program_id(0)
    first_head = step * head_count
    row, col = masks()
    decays, betas, shifted, tables = decay_tables(
        alpha_ref, beta_ref, dlog_ref, dbias_ref, first_head, head_count, parts
    )
    upper = jnp.where(row <= col, 1.0, 0.0)
    units = [(head, index) for head in range(head_count) for index in range(len(parts))]
    gain = gain_ref[...]
    root = 1.0 / math.sqrt(head_dim)
    all_cols = dproj_ref.shape[1] // 4

    def proj_cols(which, head):
        start = which * all_cols + (first_head + head) * head_dim
        return pl.ds(pl.multiple_of(start, head_dim), head_dim)

    @pl.when(step == 0)
    def _():
        dbeta_ref[...] = jnp.zeros_like(dbeta_ref)
        dalpha_ref[...] = jnp.zeros_like(dalpha_ref)
        ddlog_ref[...] = jnp.zeros_like(ddlog_ref)
        ddbias_ref[...] = jnp.zeros_like(ddbias_ref)
        dgain_ref[...] = jnp.zeros_like(dgain_ref)

    queries, key_rows, values, grads, acts, convs = {}, {}, {}, {}, {}, {}
    for head in range(head_count):
        cols = slice(head * head_dim, (head + 1) * head_dim)
        conv_q = conv_rows(query_ref[:, cols], taps_ref[0, :, cols])
        conv_k = conv_rows(key_ref[:, cols], taps_ref[1, :, cols])
        conv_v = conv_rows(value_ref[:, cols], taps_ref[2, :, cols])
        act_q = conv_q * sigmoid(conv_q)
        act_k = conv_k * sigmoid(conv_k)
        value = conv_v * sigmoid(conv_v)
        norm_q, norm_k = unit_inverse(act_q), unit_inverse(act_k)
        query, key_full = act_q * norm_q, act_k * norm_k
        convs[head] = (conv_q, conv_k, conv_v)
        acts[head] = (query, norm_q, key_full, norm_k)
        mixed = mixed_ref[:, cols]
        gate = gate_ref[:, cols]
        sig = sigmoid(gate)
        grad = grad_ref[:, cols]
        scale = lax.rsqrt(jnp.mean(mixed * mixed, axis=-1, keepdims=True) + EPSILON)
        normal = mixed * scale
        opened = gate * sig
        dgain_ref[...] += jnp.sum(grad * normal * opened, axis=0, keepdims=True)
        dproj_ref[:, proj_cols(3, head)] = (
            grad * normal * gain * (sig * (1.0 + gate * (1.0 - sig)))
        ).astype(LOW)
        grad_normal = grad * gain * opened
        grad_mixed = scale * (
            grad_normal - normal * jnp.mean(grad_normal * normal, axis=-1, keepdims=True)
        )
        for index, part in enumerate(parts):
            queries[head, index] = query[part] * root
            key_rows[head, index] = key_full[part]
            values[head, index] = value[part]
            grads[head, index] = grad_mixed[part]
    cross, scores, system, strict = {}, {}, {}, {}
    for unit in units:
        head, index = unit
        beta, _, _, _, causal = tables[head][index]
        cross[unit] = mm3(queries[unit], key_rows[unit], NT)
        scores[unit] = (cross[unit] * causal).astype(LOW)
        strict[unit] = jnp.where(row > col, beta * causal, 0.0)
        system[unit] = mm3(key_rows[unit], key_rows[unit], NT)
    grad_states = {head: None for head in range(head_count)}
    grad_q, grad_k, grad_v, gamma_grads = {}, {}, {}, {}
    grad_beta = {}
    for index in reversed(range(len(parts))):
        part = parts[index]
        for head in range(head_count):
            unit = (head, index)
            cols = slice(head * head_dim, (head + 1) * head_dim)
            beta, start, tail, last, causal = tables[head][index]
            query, key_full = queries[unit], key_rows[unit]
            query_low, key_low = query.astype(LOW), key_full.astype(LOW)
            grad = grads[unit]
            grad_low = grad.astype(LOW)
            fresh_low = fresh_ref[part, cols]
            fresh = fresh_low.astype(FULL)
            state = state_ref[head, index]
            grad_state = grad_states[head]
            grad_fresh = mm(scores[unit], grad_low, TN)
            if grad_state is not None:
                grad_state_low = grad_state.astype(LOW)
                grad_fresh = grad_fresh + mm(key_full * tail, grad_state_low)
            grad_right = mm(inverse_ref[head, index], grad_fresh, TN)
            grad_right_low = grad_right.astype(LOW)
            grad_cross = mm(grad_low, fresh_low, NT) * causal
            grad_system = -(mm(grad_right_low, fresh_low, NT) * strict[unit])
            turned = grad_cross * cross[unit] + grad_system * system[unit]
            gamma = row_sum(turned) - row_sum(turned.T)
            grad_cross_low = grad_cross.astype(LOW)
            grad_system_low = grad_system.astype(LOW)
            dquery = mm(grad_cross_low, key_low)
            dkey = (
                mm(grad_system_low, key_low)
                + mm(grad_system_low, key_low, TN)
                + mm(grad_cross_low, query_low, TN)
            )
            back = -beta * start * grad_right
            if index:
                back_low = back.astype(LOW)
                dquery = dquery + start * mm(grad_low, state, NT)
                dkey = dkey + mm(back_low, state, NT)
                gamma = gamma + row_sum(grad * start * mm(query_low, state))
                gamma = gamma + row_sum(back * mm(key_low, state))
            final = None
            if grad_state is not None:
                grad_tail = mm(fresh_low, grad_state_low, NT) * tail
                dkey = dkey + grad_tail
                tail_term = row_sum(grad_tail * key_full)
                gamma = gamma - tail_term
                final = jnp.sum(tail_term, axis=0, keepdims=True)
                if index:
                    final = final + last * jnp.sum(
                        row_sum(state.astype(FULL) * grad_state), axis=0, keepdims=True
                    )
                is_last = lax.broadcasted_iota(jnp.int32, gamma.shape, 0) == CHUNK - 1
                gamma = gamma + jnp.where(is_last, final, 0.0)
            gamma_grads[unit] = gamma
            grad_beta[unit] = (1.0 - beta) * row_sum(grad_right * fresh)
            grad_q[unit], grad_k[unit], grad_v[unit] = dquery, dkey, beta * grad_right
            if index:
                grown = mm(query * start, grad_low, TN) + mm(key_low, back_low, TN)
                if grad_state is not None:
                    grown = grown + last * grad_state
                grad_states[head] = grown
    lane = lax.broadcasted_iota(jnp.int32, (CHUNK, alpha_ref.shape[1]), 1)
    for index, part in enumerate(parts):
        gamma_cols = jnp.zeros(lane.shape, FULL)
        beta_cols = jnp.zeros(lane.shape, FULL)
        for head in range(head_count):
            gamma_cols = jnp.where(lane == first_head + head, gamma_grads[head, index], gamma_cols)
            beta_cols = jnp.where(lane == first_head + head, grad_beta[head, index], beta_cols)
        grad_decay = full_dot(upper, gamma_cols)
        grad_alpha = grad_decay * -jnp.exp(dlog_ref[...]) * sigmoid(shifted[part])
        dbeta_ref[part] += beta_cols
        dalpha_ref[part] += grad_alpha
        ddbias_ref[...] += jnp.sum(grad_alpha, axis=0, keepdims=True)
        ddlog_ref[...] += jnp.sum(grad_decay * decays[part], axis=0, keepdims=True)
    for head in range(head_count):
        cols = slice(head * head_dim, (head + 1) * head_dim)
        query, norm_q, key_full, norm_k = acts[head]
        dquery = jnp.concatenate([grad_q[head, index] for index in range(len(parts))], axis=0)
        dkey = jnp.concatenate([grad_k[head, index] for index in range(len(parts))], axis=0)
        dvalue = jnp.concatenate([grad_v[head, index] for index in range(len(parts))], axis=0)
        act_grads = (
            norm_q * root * (dquery - query * row_sum(query * dquery)),
            norm_k * (dkey - key_full * row_sum(key_full * dkey)),
            dvalue,
        )
        projected = (query_ref, key_ref, value_ref)
        for which in range(3):
            conv = convs[head][which]
            sig = sigmoid(conv)
            grad_conv = act_grads[which] * sig * (1.0 + conv * (1.0 - sig))
            grad_in, grad_taps = conv_back(
                grad_conv, projected[which][:, cols], taps_ref[which, :, cols]
            )
            dproj_ref[:, proj_cols(which, head)] = grad_in.astype(LOW)
            for tap, entry in enumerate(grad_taps):
                dtaps_ref[which, tap : tap + 1, cols] = entry


def mixer_specs(rows, heads, group, head_dim, taps_shape):
    width = group * head_dim
    wide = pl.BlockSpec((rows, width), lambda step: (0, step))
    narrow = pl.BlockSpec((rows, heads), lambda step: (0, 0))
    taps = pl.BlockSpec(taps_shape[:2] + (width,), lambda step: (0, 0, step))
    small = pl.BlockSpec((1, heads), lambda step: (0, 0))
    gain = pl.BlockSpec((1, head_dim), lambda step: (0, 0))
    chunks = rows // CHUNK
    square = pl.BlockSpec((group, chunks, CHUNK, CHUNK), lambda step: (step, 0, 0, 0))
    state = pl.BlockSpec((group, chunks, head_dim, head_dim), lambda step: (step, 0, 0, 0))
    return wide, narrow, taps, small, gain, square, state


def mixer_forward(projections, conv_taps, decay_log, decay_bias, norm_head):
    query, key_rows, value, gate, beta, alpha = projections
    rows, width = query.shape
    heads, head_dim = decay_log.shape[0], norm_head.shape[0]
    group = 2 if heads % 2 == 0 else 1
    chunks = rows // CHUNK
    wide, narrow, taps, small, gain, square, state = mixer_specs(
        rows, heads, group, head_dim, conv_taps.shape
    )
    return pl.pallas_call(
        mixer_forward_body,
        grid=(heads // group,),
        in_specs=[wide] * 4 + [narrow] * 2 + [taps, small, small, gain],
        out_specs=[wide, wide, wide, square, state],
        out_shape=[
            jax.ShapeDtypeStruct((rows, width), LOW),
            jax.ShapeDtypeStruct((rows, width), FULL),
            jax.ShapeDtypeStruct((rows, width), LOW),
            jax.ShapeDtypeStruct((heads, chunks, CHUNK, CHUNK), LOW),
            jax.ShapeDtypeStruct((heads, chunks, head_dim, head_dim), LOW),
        ],
        compiler_params=pltpu.CompilerParams(
            vmem_limit_bytes=48 * 1024 * 1024, dimension_semantics=("arbitrary",)
        ),
        name="mixer_forward",
    )(
        query, key_rows, value, gate, beta, alpha, conv_taps,
        decay_log.reshape(1, heads), decay_bias.reshape(1, heads), norm_head.reshape(1, head_dim),
    )


def mixer_backward(grad, projections, conv_taps, decay_log, decay_bias, norm_head, kept):
    query, key_rows, value, gate, beta, alpha = projections
    mixed, fresh, inverse, states = kept
    rows, width = query.shape
    heads, head_dim = decay_log.shape[0], norm_head.shape[0]
    group = 2 if heads % 2 == 0 else 1
    wide, narrow, taps, small, gain, square, state = mixer_specs(
        rows, heads, group, head_dim, conv_taps.shape
    )
    return pl.pallas_call(
        mixer_backward_body,
        grid=(heads // group,),
        in_specs=[wide] * 5
        + [narrow] * 2
        + [taps, small, small, gain, wide, wide, square, state],
        out_specs=[pl.BlockSpec((rows, 4 * width), lambda step: (0, 0))]
        + [narrow] * 2
        + [taps, small, small, gain],
        out_shape=[jax.ShapeDtypeStruct((rows, 4 * width), LOW)]
        + [jax.ShapeDtypeStruct((rows, heads), FULL)] * 2
        + [
            jax.ShapeDtypeStruct(conv_taps.shape, FULL),
            jax.ShapeDtypeStruct((1, heads), FULL),
            jax.ShapeDtypeStruct((1, heads), FULL),
            jax.ShapeDtypeStruct((1, head_dim), FULL),
        ],
        compiler_params=pltpu.CompilerParams(
            vmem_limit_bytes=48 * 1024 * 1024, dimension_semantics=("arbitrary",)
        ),
        name="mixer_backward",
    )(
        grad, query, key_rows, value, gate, beta, alpha, conv_taps,
        decay_log.reshape(1, heads), decay_bias.reshape(1, heads), norm_head.reshape(1, head_dim),
        mixed, fresh, inverse, states,
    )


def rms_scale(vector, gain):
    return vector * lax.rsqrt(jnp.mean(vector * vector, axis=-1, keepdims=True) + EPSILON) * gain


def rms_back(grad_norm, vector, gain):
    inverse = lax.rsqrt(jnp.mean(vector * vector, axis=-1, keepdims=True) + EPSILON)
    normal = vector * inverse
    scaled = grad_norm * gain
    return inverse * (scaled - normal * jnp.mean(scaled * normal, axis=-1, keepdims=True))


def scatter_steps(partial_sum):
    parts = lax.axis_size("head")
    place = lax.axis_index("head")
    own_len = partial_sum.shape[0] // parts

    def share(index):
        start = jnp.clip(index, 0, parts - 1) * own_len
        return lax.dynamic_slice_in_dim(partial_sum, start, own_len, 0).astype(FULL)

    right = left = 0.0
    for step in range(1, parts):
        right, left = yield [
            (
                (share(parts - step + place) + right).astype(LOW),
                "head",
                [(source, source + 1) for source in range(step)],
            ),
            (
                (share(step - parts + place) + left).astype(LOW),
                "head",
                [(source, source - 1) for source in range(parts - step, parts)],
            ),
        ]
        right, left = right.astype(FULL), left.astype(FULL)
    return share(place) + right + left


def gather_steps(own, buffer, micro):
    parts = lax.axis_size("head")
    place = lax.axis_index("head")
    right = left = own
    before, behind = [None] * parts, [None] * parts
    for step in range(1, parts):
        right, left = yield [
            (right, "head", [(source, source + 1) for source in range(step - 1, parts - 1)]),
            (left, "head", [(source, source - 1) for source in range(1, parts - step + 1)]),
        ]
        before[step], behind[step] = right, left
    pieces = [(own, place)]
    for step in range(1, parts):
        piece = jnp.where(place >= step, before[step], behind[parts - step])
        pieces.append((piece, lax.rem(place - step + parts, parts)))
    return placed_pieces(pieces, buffer, micro)


def offload_scatter_steps(partial_sum):
    yield from ()
    return lax.psum_scatter(partial_sum, "head", scatter_dimension=0, tiled=True).astype(FULL)


def offload_gather_steps(own, buffer, micro):
    yield from ()
    whole = lax.all_gather(own, "head", axis=0, tiled=True)
    if buffer is None:
        return whole
    buffer[0] = lax.dynamic_update_slice(buffer[0], whole[None], (micro, 0, 0))
    return buffer


def spans(size):
    masks = []
    while 1 << len(masks) < size:
        masks.append((2 << len(masks)) - 1)
    rest = [[0]]
    for mask in masks[::-1]:
        rest.append(rest[-1] + [mask ^ value for value in rest[-1]])
    return masks, rest[::-1][1:]


def pair_scatter_steps(partial_sum):
    parts = lax.axis_size("head")
    place = lax.axis_index("head")
    own_len = partial_sum.shape[0] // parts
    masks, rests = spans(parts)
    kept = {
        code: lax.dynamic_slice_in_dim(partial_sum, (place ^ code) * own_len, own_len, 0)
        for code in range(parts)
    }
    for mask, rest in zip(masks, rests):
        payload = jnp.concatenate([kept[mask ^ code].astype(LOW) for code in rest], axis=0)
        (other,) = yield [(payload, "head", [(at, at ^ mask) for at in range(parts)])]
        kept = {
            code: kept[code].astype(FULL)
            + other[index * own_len : (index + 1) * own_len].astype(FULL)
            for index, code in enumerate(rest)
        }
    return kept[0]


def pair_gather_steps(own, buffer, micro):
    parts = lax.axis_size("head")
    place = lax.axis_index("head")
    own_len = own.shape[0]
    masks, rests = spans(parts)
    kept = {0: own}
    for mask, rest in zip(masks[::-1], rests[::-1]):
        payload = jnp.concatenate([kept[code] for code in rest], axis=0)
        (other,) = yield [(payload, "head", [(at, at ^ mask) for at in range(parts)])]
        for index, code in enumerate(rest):
            kept[mask ^ code] = other[index * own_len : (index + 1) * own_len]
    return placed_pieces(
        [(kept[code], place ^ code) for code in range(parts)], buffer, micro
    )


def placed_pieces(pieces, buffer, micro):
    own_len, width = pieces[0][0].shape
    if buffer is None:
        whole = jnp.zeros((len(pieces) * own_len, width), pieces[0][0].dtype)
        for piece, index in pieces:
            whole = lax.dynamic_update_slice_in_dim(whole, piece, index * own_len, 0)
        return whole
    for piece, index in pieces:
        buffer[0] = lax.dynamic_update_slice(
            buffer[0], piece[None], (micro, index * own_len, 0)
        )
    return buffer


def butterfly_steps(value, *axes):
    for axis in axes:
        size = lax.axis_size(axis)
        bit = 1
        while bit < size:
            (other,) = yield [(value, axis, [(place, place ^ bit) for place in range(size)])]
            value = value + other
            bit *= 2
    return value


SCATTERS = dict(C=scatter_steps, P=pair_scatter_steps, S=offload_scatter_steps)
GATHERS = dict(C=gather_steps, P=pair_gather_steps, S=offload_gather_steps)
PLAN = dict(
    out="PP", mid="PP", down="PP", result="PP", grad="PP", attn="PP", inner="PP", final="PP"
)


class Flow:
    def __init__(self, steps):
        self.steps = steps
        self.result = None
        self.advance(None)

    def advance(self, received):
        try:
            self.pending = self.steps.send(received)
        except StopIteration as stop:
            self.pending = None
            self.result = stop.value


def tick(flows, work=None):
    flows[:] = [flow for flow in flows if flow.pending is not None]
    payloads = [request[0] for flow in flows for request in flow.pending]
    token = ()
    if work is not None:
        token = work(lambda value: after(value, *payloads) if payloads else value)
        token = tuple(token) if isinstance(token, (tuple, list)) else (token,)
    for flow in flows:
        received = [lax.ppermute(*request) for request in flow.pending]
        if token:
            received = lax.optimization_barrier(tuple(received) + token)[: len(received)]
        flow.advance(received)
    flows[:] = [flow for flow in flows if flow.pending is not None]


def packed(entries):
    flat = jnp.concatenate([entry.reshape(-1) for entry in entries])
    pad = -flat.shape[0] % 1024
    return jnp.pad(flat, (0, pad)).reshape(-1, 128)


def unpacked(matrix, entries):
    flat = matrix.reshape(-1)
    outs, start = [], 0
    for entry in entries:
        outs.append(flat[start : start + entry.size].reshape(entry.shape))
        start += entry.size
    return outs


def after(value, *others):
    return lax.optimization_barrier((value,) + others)[0]


def per_device(
    tokens, cotangent, lengths, norm_in, w_query, w_key, w_value, w_gate, w_beta, w_alpha,
    conv_taps, decay_log, decay_bias, norm_head, w_out, norm_mid, w_up_gate, w_up, w_down,
):
    micro_count, seq_len, model_dim = tokens.shape
    head_parts = lax.axis_size("head")
    batch_parts = lax.axis_size("batch")
    own_len = seq_len // head_parts
    first_row = lax.axis_index("head") * own_len
    positions = lax.broadcasted_iota(jnp.int32, (seq_len, 1), 0)
    in_weights = (w_query, w_key, w_value, w_gate)
    hidden_width = w_up.shape[1]
    head_width = w_query.shape[1]

    def own_of(value):
        return lax.dynamic_slice_in_dim(value, first_row, own_len, 0)

    class Micro:
        def __init__(self, micro):
            self.micro = micro
            keep = (positions < lengths[micro, 0]).astype(LOW)
            self.rows = own_of(tokens[micro]).astype(FULL)
            self.grad_rows = own_of(cotangent[micro]).astype(FULL)
            self.keep_own = own_of(keep).astype(FULL)
            self.down_grad = keep * cotangent[micro]

        def scatter(self, name, value):
            return join(Flow(SCATTERS[PLAN[name][self.micro]](value)))

        def gather(self, name, value, buffer=None):
            return join(Flow(GATHERS[PLAN[name][self.micro]](value, buffer, self.micro)))

        def project(self, tie):
            rows = tie(tokens[self.micro]).astype(FULL)
            self.normed = rms_scale(rows, norm_in).astype(LOW)
            self.projections = tuple(
                mm(self.normed, weight) for weight in in_weights + (w_beta, w_alpha)
            )
            return self.projections

        def mix(self, tie):
            query, *others = self.projections
            self.projections = (tie(query), *others)
            self.gated, *self.kept = mixer_forward(
                self.projections, conv_taps, decay_log, decay_bias, norm_head
            )
            return self.gated

        def project_out(self, tie):
            self.out_part = mm(tie(self.gated), w_out).astype(LOW)
            return self.out_part

        def after_mixer(self, out_sum):
            self.middle = self.rows + self.keep_own * out_sum
            return self.gather("mid", rms_scale(self.middle, norm_mid).astype(LOW))

        def up(self, tie):
            mid = tie(self.mid)
            self.gate_act, self.up_act = mm(mid, w_up_gate), mm(mid, w_up)
            return self.gate_act, self.up_act

        def activate(self, tie):
            gate_act, up_act = tie(self.gate_act), self.up_act
            grad_hidden = mm(self.down_grad, w_down, NT)
            sig = jax.nn.sigmoid(gate_act)
            opened = gate_act * sig
            self.hidden = (opened * up_act).astype(LOW)
            self.grad_gate = (
                grad_hidden * up_act * sig * (1.0 + gate_act * (1.0 - sig))
            ).astype(LOW)
            self.grad_up = (grad_hidden * opened).astype(LOW)
            return self.hidden, self.grad_gate, self.grad_up

        def up_back(self, tie):
            self.mid_part = (
                mm(tie(self.grad_gate), w_up_gate, NT) + mm(self.grad_up, w_up, NT)
            ).astype(LOW)
            return self.mid_part

        def down(self, tie):
            self.down_part = mm(tie(self.hidden), w_down).astype(LOW)
            return self.down_part

        def after_down(self, down_sum):
            own = (self.middle + self.keep_own * down_sum).astype(LOW)
            return self.gather("result", own, out_buffer)

        def after_up_back(self, mid_sum):
            self.gain_mid = jnp.sum(rms_scale(self.middle, 1.0) * mid_sum, axis=0)
            self.grad_middle = self.grad_rows + rms_back(mid_sum, self.middle, norm_mid)
            return self.gather("attn", (self.keep_own * self.grad_middle).astype(LOW))

        def mix_back(self, tie):
            grad_gated = mm(tie(self.attn), w_out, NT)
            self.grads, grad_beta, grad_alpha, *self.small = mixer_backward(
                grad_gated, self.projections, conv_taps, decay_log, decay_bias,
                norm_head, self.kept,
            )
            self.beta, self.alpha = grad_beta.astype(LOW), grad_alpha.astype(LOW)
            return self.grads

        def project_back(self, tie):
            grads = tie(self.grads)
            in_part = mm(self.beta, w_beta, NT) + mm(self.alpha, w_alpha, NT)
            for index, weight in enumerate(in_weights):
                in_part = in_part + mm(
                    grads[:, index * head_width : (index + 1) * head_width], weight, NT
                )
            self.in_part = in_part.astype(LOW)
            return self.in_part

        def after_project_back(self, in_sum):
            self.gain_in = jnp.sum(rms_scale(self.rows, 1.0) * in_sum, axis=0)
            own = (self.grad_middle + rms_back(in_sum, self.rows, norm_in)).astype(LOW)
            return self.gather("final", own, grad_buffer)

    flows = []
    out_buffer, grad_buffer = [jnp.zeros_like(tokens)], [jnp.zeros_like(tokens)]
    one, two = Micro(0), Micro(1)
    held = (one, two)

    def both(*names):
        return jnp.concatenate(
            [jnp.concatenate([getattr(h, name) for name in names], axis=1) for h in held], axis=0
        )

    def shared(product):
        return lax.psum_scatter(product, "batch", scatter_dimension=0, tiled=True).astype(FULL)

    def together(*works):
        return lambda tie: sum((as_tuple(work(tie)) for work in works), ())

    def as_tuple(value):
        return tuple(value) if isinstance(value, (tuple, list)) else (value,)

    def join(flow):
        flows.append(flow)
        return flow

    def until(flow, *works):
        for work in works:
            tick(flows, work)
        while flow.result is None:
            tick(flows)
        return flow.result

    product = {}

    def ff_products(tie):
        ups = mm(tie(both("mid")), both("grad_gate", "grad_up"), TN).astype(LOW)
        downs = mm(both("down_grad"), both("hidden"), TN).astype(LOW)
        product["ff"] = jnp.concatenate([ups, downs], axis=1)
        return product["ff"]

    def out_product(tie):
        product["out"] = mm(tie(both("attn")), both("gated"), TN).astype(LOW)
        return product["out"]

    def in_product(tie):
        normed = after(tie(both("normed")), share_ff)
        product["in"] = mm(normed, both("grads"), TN).astype(LOW)
        product["tiny"] = mm(both("beta", "alpha"), normed, TN)
        return product["in"], product["tiny"]

    def free(value):
        return value

    one.project(free), one.mix(free), one.project_out(free)
    flow = one.scatter("out", one.out_part)
    until(
        flow,
        lambda tie: two.project(lambda value: after(tie(value), one.out_part)),
        two.mix,
        two.project_out,
    )
    flow_two = two.scatter("out", two.out_part)
    one.mid = until(one.after_mixer(flow.result))
    flow = two.after_mixer(until(flow_two))
    tick(flows, one.up)
    tick(flows, one.activate)
    tick(flows, one.up_back)
    sum_one = one.scatter("grad", one.mid_part)
    two.mid = until(flow)
    tick(flows, one.down)
    down_one = one.scatter("down", one.down_part)
    until(sum_one, two.up, two.activate, two.up_back)
    attn_one = one.after_up_back(sum_one.result)
    sum_two = two.scatter("grad", two.mid_part)
    tick(flows, two.down)
    out_one = one.after_down(until(down_one))
    down_two = two.scatter("down", two.down_part)
    tick(flows, ff_products)
    share_ff = shared(product["ff"])
    one.attn = until(attn_one)
    attn_two = two.after_up_back(until(sum_two))
    tick(flows, one.mix_back)
    tick(flows, one.project_back)
    sum_one = one.scatter("inner", one.in_part)
    two.attn = until(attn_two)
    until(out_one)
    out_two = two.after_down(until(down_two))
    tick(flows, lambda tie: two.mix_back(lambda value: after(tie(value), one.in_part)))
    tick(flows, two.project_back)
    sum_two = two.scatter("inner", two.in_part)
    tick(flows, together(in_product, out_product))
    share_in = shared(jnp.concatenate([product["in"], product["out"]], axis=1))
    small = [a + b for a, b in zip(one.small, two.small)]
    local = (product["tiny"], small[0], small[1][0], small[2][0])
    local_flow = join(Flow(butterfly_steps(packed(local), "batch")))
    grad_one = one.after_project_back(until(sum_one))
    grad_two = two.after_project_back(until(sum_two))
    wide = (one.gain_in + two.gain_in, small[3][0], one.gain_mid + two.gain_mid)
    wide_flow = join(Flow(butterfly_steps(packed(wide), "batch", "head")))
    while flows:
        tick(flows)
    tiny, grad_taps, grad_dlog, grad_dbias = unpacked(local_flow.result, local)
    gains = unpacked(wide_flow.result, wide)
    width = model_dim // batch_parts
    tiny = lax.dynamic_slice_in_dim(tiny, lax.axis_index("batch") * width, width, 1).T
    count = w_beta.shape[1]

    def pieces(matrix, *widths):
        outs, start = [], 0
        for extent in widths:
            outs.append(matrix[:, start : start + extent])
            start += extent
        return outs

    *share_in, share_out = pieces(share_in, *([head_width] * 5))
    share_gate, share_up, share_down = pieces(share_ff, *([hidden_width] * 3))
    return (
        out_buffer[0],
        grad_buffer[0],
        gains[0], *share_in, tiny[:, :count], tiny[:, count:],
        grad_taps, grad_dlog, grad_dbias, gains[1],
        share_out.T, gains[2], share_gate, share_up, share_down.T,
    )


def solution(mesh):
    tokens, column, row = P(None, "batch", None), P(None, "head"), P("head", None)
    placed = (
        tokens, tokens, P(None, "batch"), P(), column, column, column, column, column, column,
        P(None, None, "head"), P("head"), P("head"), P(), row, P(), column, column, row,
    )
    block, turned = P("batch", "head"), P("head", "batch")
    return jax.shard_map(
        per_device,
        mesh=mesh,
        in_specs=placed,
        out_specs=(
            tokens, tokens, P(), block, block, block, block, block, block,
            P(None, None, "head"), P("head"), P("head"), P(), turned, P(), block, block, turned,
        ),
        check_vma=False,
    )
```

```python
import math

import jax
import jax.numpy as jnp
from jax import lax
from jax.experimental import pallas as pl
from jax.experimental.pallas import tpu as pltpu
from jax.sharding import PartitionSpec as P

EPSILON = 1e-06
CHUNK = 128
LOW = jnp.bfloat16
FULL = jnp.float32


def mm(left, right, dims=((1,), (0,))):
    return lax.dot_general(
        left.astype(LOW), right.astype(LOW), (dims, ((), ())), preferred_element_type=FULL
    )


NN = ((1,), (0,))
NT = ((1,), (1,))
TN = ((0,), (0,))


def mm3(left, right, dims):
    left_high = left.astype(LOW)
    left_rest = (left - left_high.astype(FULL)).astype(LOW)
    right_high = right.astype(LOW)
    right_rest = (right - right_high.astype(FULL)).astype(LOW)
    return (
        mm(left_high, right_high, dims)
        + mm(left_high, right_rest, dims)
        + mm(left_rest, right_high, dims)
    )


def row_sum(value):
    return jnp.sum(value, axis=-1, keepdims=True)


def shift_down(value, count):
    if count == 0:
        return value
    row = lax.broadcasted_iota(jnp.int32, value.shape, 0)
    return jnp.where(row >= count, pltpu.roll(value, count, 0), 0.0)


def shift_up(value, count):
    if count == 0:
        return value
    rows = value.shape[0]
    row = lax.broadcasted_iota(jnp.int32, value.shape, 0)
    return jnp.where(row < rows - count, pltpu.roll(value, rows - count, 0), 0.0)


def conv_rows(projected, taps):
    count = taps.shape[0]
    total = projected * taps[count - 1 : count]
    for tap in range(count - 1):
        total = total + shift_down(projected, count - 1 - tap) * taps[tap : tap + 1]
    return total


def conv_back(grad, projected, taps):
    count = taps.shape[0]
    grad_in = grad * taps[count - 1 : count]
    grad_taps = [None] * count
    grad_taps[count - 1] = jnp.sum(grad * projected, axis=0, keepdims=True)
    for tap in range(count - 1):
        grad_in = grad_in + shift_up(grad, count - 1 - tap) * taps[tap : tap + 1]
        grad_taps[tap] = jnp.sum(
            grad * shift_down(projected, count - 1 - tap), axis=0, keepdims=True
        )
    return grad_in, grad_taps


def column_of(matrix, index):
    lane = lax.broadcasted_iota(jnp.int32, matrix.shape, 1)
    return row_sum(jnp.where(lane == index, matrix, 0.0))


def chunk_parts(rows):
    return [slice(start, start + CHUNK) for start in range(0, rows, CHUNK)]


def masks():
    row = lax.broadcasted_iota(jnp.int32, (CHUNK, CHUNK), 0)
    col = lax.broadcasted_iota(jnp.int32, (CHUNK, CHUNK), 1)
    return row, col


def sigmoid(value):
    return 1.0 / (1.0 + jnp.exp(-value))


def softplus(value):
    return jnp.maximum(value, 0.0) + jnp.log1p(jnp.exp(-jnp.abs(value)))


def full_dot(left, right):
    return lax.dot_general(
        left,
        right,
        (((1,), (0,)), ((), ())),
        precision=lax.Precision.HIGHEST,
        preferred_element_type=FULL,
    )


def decay_tables(alpha_ref, beta_ref, dlog_ref, dbias_ref, first_head, head_count, parts):
    row, col = masks()
    lower = jnp.where(row >= col, 1.0, 0.0)
    shifted = alpha_ref[...] + dbias_ref[...]
    decays = -jnp.exp(dlog_ref[...]) * softplus(shifted)
    running = [full_dot(lower, decays[part]) for part in parts]
    betas = sigmoid(beta_ref[...])
    tables = []
    for head in range(head_count):
        beta_col = column_of(betas, first_head + head)
        per_chunk = []
        for index, part in enumerate(parts):
            gamma = column_of(running[index], first_head + head)
            spread = jnp.broadcast_to(gamma, (CHUNK, CHUNK))
            spread = spread - spread.T
            causal = jnp.where(row >= col, jnp.exp(jnp.where(row >= col, spread, 0.0)), 0.0)
            last = gamma[CHUNK - 1 : CHUNK]
            per_chunk.append(
                (beta_col[part], jnp.exp(gamma), jnp.exp(last - gamma), jnp.exp(last), causal)
            )
        tables.append(per_chunk)
    return decays, betas, shifted, tables


def unit_inverse(value):
    return lax.rsqrt(row_sum(value * value) + EPSILON)


def mixer_forward_body(
    query_ref, key_ref, value_ref, gate_ref, beta_ref, alpha_ref, taps_ref, dlog_ref, dbias_ref,
    gain_ref, gated_ref, mixed_ref, fresh_ref, inverse_ref, state_ref,
):
    rows, width = query_ref.shape
    head_dim = gain_ref.shape[1]
    head_count = width // head_dim
    parts = chunk_parts(rows)
    first_head = pl.program_id(0) * head_count
    row, col = masks()
    tables = decay_tables(
        alpha_ref, beta_ref, dlog_ref, dbias_ref, first_head, head_count, parts
    )[3]
    units = [(head, index) for head in range(head_count) for index in range(len(parts))]
    queries, key_rows, values = {}, {}, {}
    for head in range(head_count):
        cols = slice(head * head_dim, (head + 1) * head_dim)
        conv_q = conv_rows(query_ref[:, cols], taps_ref[0, :, cols])
        conv_k = conv_rows(key_ref[:, cols], taps_ref[1, :, cols])
        conv_v = conv_rows(value_ref[:, cols], taps_ref[2, :, cols])
        act_q = conv_q * sigmoid(conv_q)
        act_k = conv_k * sigmoid(conv_k)
        query = (act_q * (unit_inverse(act_q) * (1.0 / math.sqrt(head_dim)))).astype(LOW)
        key_low = (act_k * unit_inverse(act_k)).astype(LOW)
        value = conv_v * sigmoid(conv_v)
        for index, part in enumerate(parts):
            queries[head, index] = query[part]
            key_rows[head, index] = key_low[part]
            values[head, index] = value[part]
    system, scores, inverse = {}, {}, {}
    for head, index in units:
        beta, _, _, _, causal = tables[head][index]
        key_blk = key_rows[head, index]
        system[head, index] = jnp.where(row > col, beta * mm(key_blk, key_blk, NT) * causal, 0.0)
        scores[head, index] = (mm(queries[head, index], key_blk, NT) * causal).astype(LOW)
    size = 1
    while size < CHUNK:
        own = (row // (2 * size) == col // (2 * size)) & (row // size != col // size)
        for unit in units:
            part = jnp.where(own, system[unit], 0.0)
            if size == 1:
                inverse[unit] = jnp.where(row == col, 1.0, 0.0) - part
            else:
                inverse_low = inverse[unit].astype(LOW)
                inverse[unit] = inverse[unit] - mm(mm(inverse_low, part), inverse_low)
        size *= 2
    gain = gain_ref[...]
    states = {head: jnp.zeros((head_dim, head_dim), FULL) for head in range(head_count)}
    for index, part in enumerate(parts):
        for head in range(head_count):
            unit = (head, index)
            cols = slice(head * head_dim, (head + 1) * head_dim)
            beta, start, tail, last, _ = tables[head][index]
            state = states[head]
            state_ref[head, index] = state.astype(LOW)
            inverse_low = inverse[unit].astype(LOW)
            inverse_ref[head, index] = inverse_low
            right = values[unit]
            if index:
                right = right - start * mm(key_rows[unit], state)
            fresh = mm(inverse_low, beta * right)
            fresh_low = fresh.astype(LOW)
            fresh_ref[part, cols] = fresh_low
            mixed = mm(scores[unit], fresh_low)
            if index:
                mixed = mixed + start * mm(queries[unit], state)
            mixed_ref[part, cols] = mixed
            if index + 1 < len(parts):
                grown = mm(key_rows[unit].astype(FULL) * tail, fresh_low, TN)
                states[head] = last * state + grown if index else grown
            gate = gate_ref[part, cols]
            scale = lax.rsqrt(jnp.mean(mixed * mixed, axis=-1, keepdims=True) + EPSILON)
            gated_ref[part, cols] = (mixed * scale * gain * (gate * sigmoid(gate))).astype(LOW)


def mixer_backward_body(
    grad_ref, query_ref, key_ref, value_ref, gate_ref, beta_ref, alpha_ref, taps_ref, dlog_ref,
    dbias_ref, gain_ref, mixed_ref, fresh_ref, inverse_ref, state_ref,
    dproj_ref, dbeta_ref, dalpha_ref, dtaps_ref, ddlog_ref, ddbias_ref, dgain_ref,
):
    rows, width = query_ref.shape
    head_dim = gain_ref.shape[1]
    head_count = width // head_dim
    parts = chunk_parts(rows)
    step = pl.program_id(0)
    first_head = step * head_count
    row, col = masks()
    decays, betas, shifted, tables = decay_tables(
        alpha_ref, beta_ref, dlog_ref, dbias_ref, first_head, head_count, parts
    )
    upper = jnp.where(row <= col, 1.0, 0.0)
    units = [(head, index) for head in range(head_count) for index in range(len(parts))]
    gain = gain_ref[...]
    root = 1.0 / math.sqrt(head_dim)
    all_cols = dproj_ref.shape[1] // 4

    def proj_cols(which, head):
        start = which * all_cols + (first_head + head) * head_dim
        return pl.ds(pl.multiple_of(start, head_dim), head_dim)

    @pl.when(step == 0)
    def _():
        dbeta_ref[...] = jnp.zeros_like(dbeta_ref)
        dalpha_ref[...] = jnp.zeros_like(dalpha_ref)
        ddlog_ref[...] = jnp.zeros_like(ddlog_ref)
        ddbias_ref[...] = jnp.zeros_like(ddbias_ref)
        dgain_ref[...] = jnp.zeros_like(dgain_ref)

    queries, key_rows, values, grads, acts, convs = {}, {}, {}, {}, {}, {}
    for head in range(head_count):
        cols = slice(head * head_dim, (head + 1) * head_dim)
        conv_q = conv_rows(query_ref[:, cols], taps_ref[0, :, cols])
        conv_k = conv_rows(key_ref[:, cols], taps_ref[1, :, cols])
        conv_v = conv_rows(value_ref[:, cols], taps_ref[2, :, cols])
        act_q = conv_q * sigmoid(conv_q)
        act_k = conv_k * sigmoid(conv_k)
        value = conv_v * sigmoid(conv_v)
        norm_q, norm_k = unit_inverse(act_q), unit_inverse(act_k)
        query, key_full = act_q * norm_q, act_k * norm_k
        convs[head] = (conv_q, conv_k, conv_v)
        acts[head] = (query, norm_q, key_full, norm_k)
        mixed = mixed_ref[:, cols]
        gate = gate_ref[:, cols]
        sig = sigmoid(gate)
        grad = grad_ref[:, cols]
        scale = lax.rsqrt(jnp.mean(mixed * mixed, axis=-1, keepdims=True) + EPSILON)
        normal = mixed * scale
        opened = gate * sig
        dgain_ref[...] += jnp.sum(grad * normal * opened, axis=0, keepdims=True)
        dproj_ref[:, proj_cols(3, head)] = (
            grad * normal * gain * (sig * (1.0 + gate * (1.0 - sig)))
        ).astype(LOW)
        grad_normal = grad * gain * opened
        grad_mixed = scale * (
            grad_normal - normal * jnp.mean(grad_normal * normal, axis=-1, keepdims=True)
        )
        for index, part in enumerate(parts):
            queries[head, index] = query[part] * root
            key_rows[head, index] = key_full[part]
            values[head, index] = value[part]
            grads[head, index] = grad_mixed[part]
    cross, scores, system, strict = {}, {}, {}, {}
    for unit in units:
        head, index = unit
        beta, _, _, _, causal = tables[head][index]
        cross[unit] = mm3(queries[unit], key_rows[unit], NT)
        scores[unit] = (cross[unit] * causal).astype(LOW)
        strict[unit] = jnp.where(row > col, beta * causal, 0.0)
        system[unit] = mm3(key_rows[unit], key_rows[unit], NT)
    grad_states = {head: None for head in range(head_count)}
    grad_q, grad_k, grad_v, gamma_grads = {}, {}, {}, {}
    grad_beta = {}
    for index in reversed(range(len(parts))):
        part = parts[index]
        for head in range(head_count):
            unit = (head, index)
            cols = slice(head * head_dim, (head + 1) * head_dim)
            beta, start, tail, last, causal = tables[head][index]
            query, key_full = queries[unit], key_rows[unit]
            query_low, key_low = query.astype(LOW), key_full.astype(LOW)
            grad = grads[unit]
            grad_low = grad.astype(LOW)
            fresh_low = fresh_ref[part, cols]
            fresh = fresh_low.astype(FULL)
            state = state_ref[head, index]
            grad_state = grad_states[head]
            grad_fresh = mm(scores[unit], grad_low, TN)
            if grad_state is not None:
                grad_state_low = grad_state.astype(LOW)
                grad_fresh = grad_fresh + mm(key_full * tail, grad_state_low)
            grad_right = mm(inverse_ref[head, index], grad_fresh, TN)
            grad_right_low = grad_right.astype(LOW)
            grad_cross = mm(grad_low, fresh_low, NT) * causal
            grad_system = -(mm(grad_right_low, fresh_low, NT) * strict[unit])
            turned = grad_cross * cross[unit] + grad_system * system[unit]
            gamma = row_sum(turned) - row_sum(turned.T)
            grad_cross_low = grad_cross.astype(LOW)
            grad_system_low = grad_system.astype(LOW)
            dquery = mm(grad_cross_low, key_low)
            dkey = (
                mm(grad_system_low, key_low)
                + mm(grad_system_low, key_low, TN)
                + mm(grad_cross_low, query_low, TN)
            )
            back = -beta * start * grad_right
            if index:
                back_low = back.astype(LOW)
                dquery = dquery + start * mm(grad_low, state, NT)
                dkey = dkey + mm(back_low, state, NT)
                gamma = gamma + row_sum(grad * start * mm(query_low, state))
                gamma = gamma + row_sum(back * mm(key_low, state))
            final = None
            if grad_state is not None:
                grad_tail = mm(fresh_low, grad_state_low, NT) * tail
                dkey = dkey + grad_tail
                tail_term = row_sum(grad_tail * key_full)
                gamma = gamma - tail_term
                final = jnp.sum(tail_term, axis=0, keepdims=True)
                if index:
                    final = final + last * jnp.sum(
                        row_sum(state.astype(FULL) * grad_state), axis=0, keepdims=True
                    )
                is_last = lax.broadcasted_iota(jnp.int32, gamma.shape, 0) == CHUNK - 1
                gamma = gamma + jnp.where(is_last, final, 0.0)
            gamma_grads[unit] = gamma
            grad_beta[unit] = (1.0 - beta) * row_sum(grad_right * fresh)
            grad_q[unit], grad_k[unit], grad_v[unit] = dquery, dkey, beta * grad_right
            if index:
                grown = mm(query * start, grad_low, TN) + mm(key_low, back_low, TN)
                if grad_state is not None:
                    grown = grown + last * grad_state
                grad_states[head] = grown
    lane = lax.broadcasted_iota(jnp.int32, (CHUNK, alpha_ref.shape[1]), 1)
    for index, part in enumerate(parts):
        gamma_cols = jnp.zeros(lane.shape, FULL)
        beta_cols = jnp.zeros(lane.shape, FULL)
        for head in range(head_count):
            gamma_cols = jnp.where(lane == first_head + head, gamma_grads[head, index], gamma_cols)
            beta_cols = jnp.where(lane == first_head + head, grad_beta[head, index], beta_cols)
        grad_decay = full_dot(upper, gamma_cols)
        grad_alpha = grad_decay * -jnp.exp(dlog_ref[...]) * sigmoid(shifted[part])
        dbeta_ref[part] += beta_cols
        dalpha_ref[part] += grad_alpha
        ddbias_ref[...] += jnp.sum(grad_alpha, axis=0, keepdims=True)
        ddlog_ref[...] += jnp.sum(grad_decay * decays[part], axis=0, keepdims=True)
    for head in range(head_count):
        cols = slice(head * head_dim, (head + 1) * head_dim)
        query, norm_q, key_full, norm_k = acts[head]
        dquery = jnp.concatenate([grad_q[head, index] for index in range(len(parts))], axis=0)
        dkey = jnp.concatenate([grad_k[head, index] for index in range(len(parts))], axis=0)
        dvalue = jnp.concatenate([grad_v[head, index] for index in range(len(parts))], axis=0)
        act_grads = (
            norm_q * root * (dquery - query * row_sum(query * dquery)),
            norm_k * (dkey - key_full * row_sum(key_full * dkey)),
            dvalue,
        )
        projected = (query_ref, key_ref, value_ref)
        for which in range(3):
            conv = convs[head][which]
            sig = sigmoid(conv)
            grad_conv = act_grads[which] * sig * (1.0 + conv * (1.0 - sig))
            grad_in, grad_taps = conv_back(
                grad_conv, projected[which][:, cols], taps_ref[which, :, cols]
            )
            dproj_ref[:, proj_cols(which, head)] = grad_in.astype(LOW)
            for tap, entry in enumerate(grad_taps):
                dtaps_ref[which, tap : tap + 1, cols] = entry


def mixer_specs(rows, heads, group, head_dim, taps_shape):
    width = group * head_dim
    wide = pl.BlockSpec((rows, width), lambda step: (0, step))
    narrow = pl.BlockSpec((rows, heads), lambda step: (0, 0))
    taps = pl.BlockSpec(taps_shape[:2] + (width,), lambda step: (0, 0, step))
    small = pl.BlockSpec((1, heads), lambda step: (0, 0))
    gain = pl.BlockSpec((1, head_dim), lambda step: (0, 0))
    chunks = rows // CHUNK
    square = pl.BlockSpec((group, chunks, CHUNK, CHUNK), lambda step: (step, 0, 0, 0))
    state = pl.BlockSpec((group, chunks, head_dim, head_dim), lambda step: (step, 0, 0, 0))
    return wide, narrow, taps, small, gain, square, state


def mixer_forward(projections, conv_taps, decay_log, decay_bias, norm_head):
    query, key_rows, value, gate, beta, alpha = projections
    rows, width = query.shape
    heads, head_dim = decay_log.shape[0], norm_head.shape[0]
    group = 2 if heads % 2 == 0 else 1
    chunks = rows // CHUNK
    wide, narrow, taps, small, gain, square, state = mixer_specs(
        rows, heads, group, head_dim, conv_taps.shape
    )
    return pl.pallas_call(
        mixer_forward_body,
        grid=(heads // group,),
        in_specs=[wide] * 4 + [narrow] * 2 + [taps, small, small, gain],
        out_specs=[wide, wide, wide, square, state],
        out_shape=[
            jax.ShapeDtypeStruct((rows, width), LOW),
            jax.ShapeDtypeStruct((rows, width), FULL),
            jax.ShapeDtypeStruct((rows, width), LOW),
            jax.ShapeDtypeStruct((heads, chunks, CHUNK, CHUNK), LOW),
            jax.ShapeDtypeStruct((heads, chunks, head_dim, head_dim), LOW),
        ],
        compiler_params=pltpu.CompilerParams(
            vmem_limit_bytes=48 * 1024 * 1024, dimension_semantics=("arbitrary",)
        ),
        name="mixer_forward",
    )(
        query, key_rows, value, gate, beta, alpha, conv_taps,
        decay_log.reshape(1, heads), decay_bias.reshape(1, heads), norm_head.reshape(1, head_dim),
    )


def mixer_backward(grad, projections, conv_taps, decay_log, decay_bias, norm_head, kept):
    query, key_rows, value, gate, beta, alpha = projections
    mixed, fresh, inverse, states = kept
    rows, width = query.shape
    heads, head_dim = decay_log.shape[0], norm_head.shape[0]
    group = 2 if heads % 2 == 0 else 1
    wide, narrow, taps, small, gain, square, state = mixer_specs(
        rows, heads, group, head_dim, conv_taps.shape
    )
    return pl.pallas_call(
        mixer_backward_body,
        grid=(heads // group,),
        in_specs=[wide] * 5
        + [narrow] * 2
        + [taps, small, small, gain, wide, wide, square, state],
        out_specs=[pl.BlockSpec((rows, 4 * width), lambda step: (0, 0))]
        + [narrow] * 2
        + [taps, small, small, gain],
        out_shape=[jax.ShapeDtypeStruct((rows, 4 * width), LOW)]
        + [jax.ShapeDtypeStruct((rows, heads), FULL)] * 2
        + [
            jax.ShapeDtypeStruct(conv_taps.shape, FULL),
            jax.ShapeDtypeStruct((1, heads), FULL),
            jax.ShapeDtypeStruct((1, heads), FULL),
            jax.ShapeDtypeStruct((1, head_dim), FULL),
        ],
        compiler_params=pltpu.CompilerParams(
            vmem_limit_bytes=48 * 1024 * 1024, dimension_semantics=("arbitrary",)
        ),
        name="mixer_backward",
    )(
        grad, query, key_rows, value, gate, beta, alpha, conv_taps,
        decay_log.reshape(1, heads), decay_bias.reshape(1, heads), norm_head.reshape(1, head_dim),
        mixed, fresh, inverse, states,
    )


def rms_scale(vector, gain):
    return vector * lax.rsqrt(jnp.mean(vector * vector, axis=-1, keepdims=True) + EPSILON) * gain


def rms_back(grad_norm, vector, gain):
    inverse = lax.rsqrt(jnp.mean(vector * vector, axis=-1, keepdims=True) + EPSILON)
    normal = vector * inverse
    scaled = grad_norm * gain
    return inverse * (scaled - normal * jnp.mean(scaled * normal, axis=-1, keepdims=True))


def codes(parts):
    masks = []
    while 1 << len(masks) < parts:
        masks.append((2 << len(masks)) - 1)
    order = []
    for code in range(parts):
        place = 0
        for index, mask in enumerate(masks):
            if code >> (len(masks) - 1 - index) & 1:
                place ^= mask
        order.append(place)
    return masks, order


def own_code():
    order = codes(lax.axis_size("head"))[1]
    place = lax.axis_index("head")
    return sum(jnp.where(place == at, code, 0) for code, at in enumerate(order))


def scatter_steps(partial_sum):
    parts = lax.axis_size("head")
    code = own_code()
    for mask in codes(parts)[0]:
        half = partial_sum.shape[0] // 2
        parts //= 2
        bit = lax.rem(code // parts, 2)
        payload = lax.dynamic_slice_in_dim(partial_sum, (1 - bit) * half, half, 0)
        kept = lax.dynamic_slice_in_dim(partial_sum, bit * half, half, 0)
        pairs = [(at, at ^ mask) for at in range(lax.axis_size("head"))]
        (other,) = yield [(payload.astype(LOW), "head", pairs)]
        partial_sum = kept.astype(FULL) + other.astype(FULL)
    return partial_sum


def gather_steps(own, buffer=None, micro=0):
    parts = lax.axis_size("head")
    code = own_code()
    step = 1
    for mask in codes(parts)[0][::-1]:
        (other,) = yield [(own, "head", [(at, at ^ mask) for at in range(parts)])]
        bit = lax.rem(code // step, 2)
        size = own.shape[0]
        step *= 2
        if buffer is not None and step == parts:
            for piece, index in ((own, bit), (other, 1 - bit)):
                buffer[0] = lax.dynamic_update_slice(
                    buffer[0], piece[None], (micro, index * size, 0)
                )
            return buffer
        shape = list(own.shape)
        shape[0] *= 2
        joined = jnp.zeros(shape, own.dtype)
        joined = lax.dynamic_update_slice_in_dim(joined, own, bit * size, 0)
        own = lax.dynamic_update_slice_in_dim(joined, other, (1 - bit) * size, 0)
    return own


OUTER, INNER, BACK = [(0, 1), (3, 2)], [(1, 2), (2, 1)], [(1, 0), (2, 3)]


def hub_scatter_steps(partial_sum):
    half = partial_sum.shape[0] // 2
    bit = lax.axis_index("head") // 2
    near = lax.dynamic_slice_in_dim(partial_sum, bit * half, half, 0)
    far = lax.dynamic_slice_in_dim(partial_sum, (1 - bit) * half, half, 0)
    (first,) = yield [(far, "head", OUTER)]
    passed = (far.astype(FULL) + first.astype(FULL)).astype(LOW)
    second, last = yield [(passed, "head", INNER), (near, "head", OUTER)]
    return near.astype(FULL) + second.astype(FULL) + last.astype(FULL)


def hub_gather_steps(own, buffer=None, micro=0):
    half, width = own.shape
    place = lax.axis_index("head")
    bit = place // 2
    middle = (place == 1) | (place == 2)
    other, near = yield [(own, "head", INNER), (own, "head", BACK)]
    (far,) = yield [(other, "head", BACK)]
    pieces = (jnp.where(middle, own, near), bit), (jnp.where(middle, other, far), 1 - bit)
    if buffer is None:
        whole = jnp.zeros((2 * half, width), own.dtype)
        for piece, index in pieces:
            whole = lax.dynamic_update_slice_in_dim(whole, piece, index * half, 0)
        return whole
    for piece, index in pieces:
        buffer[0] = lax.dynamic_update_slice(buffer[0], piece[None], (micro, index * half, 0))
    return buffer


def batch_scatter_steps(value):
    size = lax.axis_size("batch")
    place = lax.axis_index("batch")
    while size > 1:
        size //= 2
        half = value.shape[0] // 2
        bit = lax.rem(place // size, 2)
        payload = lax.dynamic_slice_in_dim(value, (1 - bit) * half, half, 0)
        kept = lax.dynamic_slice_in_dim(value, bit * half, half, 0)
        (other,) = yield [
            (payload.astype(LOW), "batch", [(at, at ^ size) for at in range(lax.axis_size("batch"))])
        ]
        value = kept.astype(FULL) + other.astype(FULL)
    return value


def butterfly_steps(local, wide):
    for axis in ("batch", "head"):
        size = lax.axis_size(axis)
        bit = 1
        while bit < size:
            value = jnp.concatenate([local, wide], axis=0) if axis == "batch" else wide
            (other,) = yield [(value, axis, [(at, at ^ bit) for at in range(size)])]
            value = value + other
            if axis == "batch":
                local, wide = value[: local.shape[0]], value[local.shape[0] :]
            else:
                wide = value
            bit *= 2
    return local, wide


LAG = 2


class Flow:
    def __init__(self, steps, lag=0):
        self.steps = steps
        self.lag = lag
        self.fresh = True
        self.result = None
        self.advance(None)

    def advance(self, received):
        self.fresh = True
        try:
            self.pending = self.steps.send(received)
        except StopIteration as stop:
            self.pending = None
            self.result = stop.value


class Clock:
    def __init__(self):
        self.flows = []
        self.due = []

    def join(self, steps, lag=0):
        flow = Flow(steps, lag)
        self.flows.append(flow)
        return flow

    def step(self, work=None):
        flows = [flow for flow in self.flows if flow.pending is not None]
        for flow in flows:
            self.due.extend([flow.lag, request[0]] for request in flow.pending)
        token = ()
        if work is not None:
            ahead = [value for lag, value in self.due if lag <= 0]
            token = work(lambda value: after(value, *ahead) if ahead else value)
            token = tuple(token) if isinstance(token, (tuple, list)) else (token,)
            self.due = [[lag - 1, value] for lag, value in self.due if lag > 0]
        for flow in flows:
            received = [lax.ppermute(*request) for request in flow.pending]
            if token:
                received = lax.optimization_barrier(tuple(received) + token)[: len(received)]
            flow.advance(received)
            if flow.pending is None:
                self.due.extend([flow.lag, value] for value in received)
        self.flows = [flow for flow in flows if flow.pending is not None]

    def until(self, flow):
        while flow.result is None:
            self.step()
        return flow.result


def packed(entries):
    flat = jnp.concatenate([entry.reshape(-1) for entry in entries])
    pad = -flat.shape[0] % 1024
    return jnp.pad(flat, (0, pad)).reshape(-1, 128)


def unpacked(matrix, entries):
    flat = matrix.reshape(-1)
    outs, start = [], 0
    for entry in entries:
        outs.append(flat[start : start + entry.size].reshape(entry.shape))
        start += entry.size
    return outs


def after(value, *others):
    return lax.optimization_barrier((value,) + others)[0]


def per_device(
    tokens, cotangent, lengths, norm_in, w_query, w_key, w_value, w_gate, w_beta, w_alpha,
    conv_taps, decay_log, decay_bias, norm_head, w_out, norm_mid, w_up_gate, w_up, w_down,
):
    micro_count, seq_len, model_dim = tokens.shape
    head_parts = lax.axis_size("head")
    batch_parts = lax.axis_size("batch")
    hub = False
    place = lax.axis_index("head")
    if hub:
        own_len = seq_len // 2
        first_row = place // 2 * own_len
        counts = jnp.where((place == 1) | (place == 2), 1.0, 0.0)
        scatter, gather = hub_scatter_steps, hub_gather_steps
    else:
        own_len = seq_len // head_parts
        first_row = own_code() * own_len
        counts = 1.0
        scatter, gather = scatter_steps, gather_steps
    positions = lax.broadcasted_iota(jnp.int32, (seq_len, 1), 0)
    in_weights = (w_query, w_key, w_value, w_gate)
    hidden_width = w_up.shape[1]
    head_width = w_query.shape[1]

    def own_of(value):
        return lax.dynamic_slice_in_dim(value, first_row, own_len, 0)

    class Micro:
        def __init__(self, micro):
            self.micro = micro
            keep = (positions < lengths[micro, 0]).astype(LOW)
            self.rows = own_of(tokens[micro]).astype(FULL)
            self.grad_rows = own_of(cotangent[micro]).astype(FULL)
            self.keep_own = own_of(keep).astype(FULL)
            self.down_grad = keep * cotangent[micro]


        def project(self, tie):
            rows = tie(tokens[self.micro]).astype(FULL)
            self.normed = rms_scale(rows, norm_in).astype(LOW)
            self.projections = tuple(
                mm(self.normed, weight) for weight in in_weights + (w_beta, w_alpha)
            )
            return self.projections

        def mix(self, tie):
            query, *others = self.projections
            self.projections = (tie(query), *others)
            self.gated, *self.kept = mixer_forward(
                self.projections, conv_taps, decay_log, decay_bias, norm_head
            )
            return self.gated

        def project_out(self, tie):
            self.out_part = mm(tie(self.gated), w_out).astype(LOW)
            return self.out_part

        def after_mixer(self, out_sum):
            self.middle = self.rows + self.keep_own * out_sum
            return join(gather(rms_scale(self.middle, norm_mid).astype(LOW)))

        def up(self, tie):
            mid = tie(self.mid)
            self.gate_act, self.up_act = mm(mid, w_up_gate), mm(mid, w_up)
            return self.gate_act, self.up_act

        def activate(self, tie):
            gate_act, up_act = tie(self.gate_act), self.up_act
            grad_hidden = mm(self.down_grad, w_down, NT)
            sig = jax.nn.sigmoid(gate_act)
            opened = gate_act * sig
            self.hidden = (opened * up_act).astype(LOW)
            self.grad_gate = (
                grad_hidden * up_act * sig * (1.0 + gate_act * (1.0 - sig))
            ).astype(LOW)
            self.grad_up = (grad_hidden * opened).astype(LOW)
            return self.hidden, self.grad_gate, self.grad_up

        def up_back(self, tie):
            self.mid_part = (
                mm(tie(self.grad_gate), w_up_gate, NT) + mm(self.grad_up, w_up, NT)
            ).astype(LOW)
            return self.mid_part

        def down(self, tie):
            self.down_part = mm(tie(self.hidden), w_down).astype(LOW)
            return self.down_part

        def after_down(self, down_sum):
            own = (self.middle + self.keep_own * down_sum).astype(LOW)
            return join(gather(own, out_buffer, self.micro), LAG)

        def after_up_back(self, mid_sum):
            self.gain_mid = counts * jnp.sum(rms_scale(self.middle, 1.0) * mid_sum, axis=0)
            self.grad_middle = self.grad_rows + rms_back(mid_sum, self.middle, norm_mid)
            return join(gather((self.keep_own * self.grad_middle).astype(LOW)))

        def mix_back(self, tie):
            grad_gated = mm(tie(self.attn), w_out, NT)
            self.grads, grad_beta, grad_alpha, *self.small = mixer_backward(
                grad_gated, self.projections, conv_taps, decay_log, decay_bias,
                norm_head, self.kept,
            )
            self.beta, self.alpha = grad_beta.astype(LOW), grad_alpha.astype(LOW)
            return self.grads

        def project_back(self, tie):
            grads = tie(self.grads)
            in_part = mm(self.beta, w_beta, NT) + mm(self.alpha, w_alpha, NT)
            for index, weight in enumerate(in_weights):
                in_part = in_part + mm(
                    grads[:, index * head_width : (index + 1) * head_width], weight, NT
                )
            self.in_part = in_part.astype(LOW)
            rows = tokens[self.micro].astype(FULL)
            self.gain_in = jnp.sum(rms_scale(rows, 1.0) * in_part, axis=0)
            return self.in_part, self.gain_in

        def after_project_back(self, in_sum):
            own = (self.grad_middle + rms_back(in_sum, self.rows, norm_in)).astype(LOW)
            return join(gather(own, grad_buffer, self.micro), LAG)

    clock = Clock()
    join, step, until = clock.join, clock.step, clock.until
    out_buffer, grad_buffer = [jnp.zeros_like(tokens)], [jnp.zeros_like(tokens)]
    one, two = Micro(0), Micro(1)
    held = (one, two)

    def both(*names):
        return jnp.concatenate(
            [jnp.concatenate([getattr(h, name) for name in names], axis=1) for h in held], axis=0
        )

    def shared(product):
        return lax.psum_scatter(product, "batch", scatter_dimension=0, tiled=True)

    def together(*works):
        def run(tie):
            token = ()
            for work in works:
                value = work(tie)
                token += tuple(value) if isinstance(value, (tuple, list)) else (value,)
            return token

        return run

    product = {}

    def ups_product(tie):
        product["ups"] = mm(tie(both("mid")), both("grad_gate", "grad_up"), TN).astype(LOW)
        return product["ups"]

    def downs_product(tie):
        downs = mm(tie(both("down_grad")), both("hidden"), TN).astype(LOW)
        product["ff"] = jnp.concatenate([product["ups"], downs], axis=1)
        return product["ff"]

    def out_product(tie):
        product["out"] = mm(tie(both("attn")), both("gated"), TN).astype(LOW)
        return product["out"]

    def in_product(tie):
        normed = after(tie(both("normed")), share_ff)
        product["in"] = mm(normed, both("grads"), TN).astype(LOW)
        product["tiny"] = mm(both("beta", "alpha"), normed, TN)
        return product["in"], product["tiny"]

    def free(value):
        return value

    one.project(free), one.mix(free), one.project_out(free)
    sum_one = join(scatter(one.out_part))
    step(lambda tie: two.project(lambda value: after(tie(value), one.out_part)))
    step(two.mix)
    until(sum_one)
    mid_one = one.after_mixer(sum_one.result)
    two.project_out(free)
    sum_two = join(scatter(two.out_part))
    one.mid = until(mid_one)
    mid_two = two.after_mixer(until(sum_two))
    step(one.up)
    step(together(one.activate, one.up_back))
    sum_one = join(scatter(one.mid_part))
    two.mid = until(mid_two)
    step(together(one.down, two.up))
    down_one = join(scatter(one.down_part), LAG)
    step(together(two.activate, two.up_back))
    attn_one = one.after_up_back(until(sum_one))
    sum_two = join(scatter(two.mid_part))
    step(ups_product)
    step(together(downs_product, two.down))
    share_ff = shared(product["ff"])
    out_one = one.after_down(until(down_one))
    one.attn = until(attn_one)
    attn_two = two.after_up_back(until(sum_two))
    down_two = join(scatter(two.down_part), LAG)
    step(one.mix_back)
    step(one.project_back)
    sum_one = join(scatter(one.in_part), LAG)
    two.attn = until(attn_two)
    step(
        together(
            out_product, lambda tie: two.mix_back(lambda value: after(tie(value), one.in_part))
        )
    )
    out_flow = join(batch_scatter_steps(product["out"]), LAG)
    step(in_product)
    share_in = shared(product["in"])
    step(two.project_back)
    sum_two = join(scatter(two.in_part))
    small = [a + b for a, b in zip(one.small, two.small)]
    local = (product["tiny"], small[0], small[1][0], small[2][0])
    wide = (one.gain_in + two.gain_in, small[3][0], one.gain_mid + two.gain_mid)
    small_flow = join(butterfly_steps(packed(local), packed(wide)))
    out_two = two.after_down(until(down_two))
    grad_one = one.after_project_back(until(sum_one))
    grad_two = two.after_project_back(until(sum_two))
    while clock.flows:
        step()
    tiny, grad_taps, grad_dlog, grad_dbias = unpacked(small_flow.result[0], local)
    gains = unpacked(small_flow.result[1], wide)
    width = model_dim // batch_parts
    tiny = lax.dynamic_slice_in_dim(tiny, lax.axis_index("batch") * width, width, 1).T
    count = w_beta.shape[1]

    def pieces(matrix, *widths):
        outs, start = [], 0
        for extent in widths:
            outs.append(matrix[:, start : start + extent].astype(FULL))
            start += extent
        return outs

    share_in = pieces(share_in, *([head_width] * 4))
    share_gate, share_up, share_down = pieces(share_ff, *([hidden_width] * 3))
    return (
        out_buffer[0],
        grad_buffer[0],
        gains[0], *share_in, tiny[:, :count], tiny[:, count:],
        grad_taps, grad_dlog, grad_dbias, gains[1],
        out_flow.result.T, gains[2], share_gate, share_up, share_down.T,
    )


def solution(mesh):
    tokens, column, row = P(None, "batch", None), P(None, "head"), P("head", None)
    placed = (
        tokens, tokens, P(None, "batch"), P(), column, column, column, column, column, column,
        P(None, None, "head"), P("head"), P("head"), P(), row, P(), column, column, row,
    )
    block, turned = P("batch", "head"), P("head", "batch")
    return jax.shard_map(
        per_device,
        mesh=mesh,
        in_specs=placed,
        out_specs=(
            tokens, tokens, P(), block, block, block, block, block, block,
            P(None, None, "head"), P("head"), P("head"), P(), turned, P(), block, block, turned,
        ),
        check_vma=False,
    )
```

```python
import math

import jax
import jax.numpy as jnp
from jax import lax
from jax.experimental import pallas as pl
from jax.experimental.pallas import tpu as pltpu
from jax.sharding import PartitionSpec as P

EPSILON = 1e-06
CHUNK = 128
LOW = jnp.bfloat16
FULL = jnp.float32


def mm(left, right, dims=((1,), (0,))):
    return lax.dot_general(
        left.astype(LOW), right.astype(LOW), (dims, ((), ())), preferred_element_type=FULL
    )


NN = ((1,), (0,))
NT = ((1,), (1,))
TN = ((0,), (0,))


def mm3(left, right, dims):
    left_high = left.astype(LOW)
    left_rest = (left - left_high.astype(FULL)).astype(LOW)
    right_high = right.astype(LOW)
    right_rest = (right - right_high.astype(FULL)).astype(LOW)
    return (
        mm(left_high, right_high, dims)
        + mm(left_high, right_rest, dims)
        + mm(left_rest, right_high, dims)
    )


def row_sum(value):
    return jnp.sum(value, axis=-1, keepdims=True)


def shift_down(value, count):
    if count == 0:
        return value
    row = lax.broadcasted_iota(jnp.int32, value.shape, 0)
    return jnp.where(row >= count, pltpu.roll(value, count, 0), 0.0)


def shift_up(value, count):
    if count == 0:
        return value
    rows = value.shape[0]
    row = lax.broadcasted_iota(jnp.int32, value.shape, 0)
    return jnp.where(row < rows - count, pltpu.roll(value, rows - count, 0), 0.0)


def conv_rows(projected, taps):
    count = taps.shape[0]
    total = projected * taps[count - 1 : count]
    for tap in range(count - 1):
        total = total + shift_down(projected, count - 1 - tap) * taps[tap : tap + 1]
    return total


def conv_back(grad, projected, taps):
    count = taps.shape[0]
    grad_in = grad * taps[count - 1 : count]
    grad_taps = [None] * count
    grad_taps[count - 1] = jnp.sum(grad * projected, axis=0, keepdims=True)
    for tap in range(count - 1):
        grad_in = grad_in + shift_up(grad, count - 1 - tap) * taps[tap : tap + 1]
        grad_taps[tap] = jnp.sum(
            grad * shift_down(projected, count - 1 - tap), axis=0, keepdims=True
        )
    return grad_in, grad_taps


def column_of(matrix, index):
    lane = lax.broadcasted_iota(jnp.int32, matrix.shape, 1)
    return row_sum(jnp.where(lane == index, matrix, 0.0))


def chunk_parts(rows):
    return [slice(start, start + CHUNK) for start in range(0, rows, CHUNK)]


def masks():
    row = lax.broadcasted_iota(jnp.int32, (CHUNK, CHUNK), 0)
    col = lax.broadcasted_iota(jnp.int32, (CHUNK, CHUNK), 1)
    return row, col


def sigmoid(value):
    return 1.0 / (1.0 + jnp.exp(-value))


def softplus(value):
    return jnp.maximum(value, 0.0) + jnp.log1p(jnp.exp(-jnp.abs(value)))


def full_dot(left, right):
    return lax.dot_general(
        left,
        right,
        (((1,), (0,)), ((), ())),
        precision=lax.Precision.HIGHEST,
        preferred_element_type=FULL,
    )


def decay_tables(alpha_ref, beta_ref, dlog_ref, dbias_ref, first_head, head_count, parts):
    row, col = masks()
    lower = jnp.where(row >= col, 1.0, 0.0)
    shifted = alpha_ref[...] + dbias_ref[...]
    decays = -jnp.exp(dlog_ref[...]) * softplus(shifted)
    running = [full_dot(lower, decays[part]) for part in parts]
    betas = sigmoid(beta_ref[...])
    tables = []
    for head in range(head_count):
        beta_col = column_of(betas, first_head + head)
        per_chunk = []
        for index, part in enumerate(parts):
            gamma = column_of(running[index], first_head + head)
            spread = jnp.broadcast_to(gamma, (CHUNK, CHUNK))
            spread = spread - spread.T
            causal = jnp.where(row >= col, jnp.exp(jnp.where(row >= col, spread, 0.0)), 0.0)
            last = gamma[CHUNK - 1 : CHUNK]
            per_chunk.append(
                (beta_col[part], jnp.exp(gamma), jnp.exp(last - gamma), jnp.exp(last), causal)
            )
        tables.append(per_chunk)
    return decays, betas, shifted, tables


def unit_inverse(value):
    return lax.rsqrt(row_sum(value * value) + EPSILON)


def mixer_forward_body(
    query_ref, key_ref, value_ref, gate_ref, beta_ref, alpha_ref, taps_ref, dlog_ref, dbias_ref,
    gain_ref, gated_ref, mixed_ref, fresh_ref, inverse_ref, state_ref,
):
    rows, width = query_ref.shape
    head_dim = gain_ref.shape[1]
    head_count = width // head_dim
    parts = chunk_parts(rows)
    first_head = pl.program_id(0) * head_count
    row, col = masks()
    tables = decay_tables(
        alpha_ref, beta_ref, dlog_ref, dbias_ref, first_head, head_count, parts
    )[3]
    units = [(head, index) for head in range(head_count) for index in range(len(parts))]
    queries, key_rows, values = {}, {}, {}
    for head in range(head_count):
        cols = slice(head * head_dim, (head + 1) * head_dim)
        conv_q = conv_rows(query_ref[:, cols], taps_ref[0, :, cols])
        conv_k = conv_rows(key_ref[:, cols], taps_ref[1, :, cols])
        conv_v = conv_rows(value_ref[:, cols], taps_ref[2, :, cols])
        act_q = conv_q * sigmoid(conv_q)
        act_k = conv_k * sigmoid(conv_k)
        query = (act_q * (unit_inverse(act_q) * (1.0 / math.sqrt(head_dim)))).astype(LOW)
        key_low = (act_k * unit_inverse(act_k)).astype(LOW)
        value = conv_v * sigmoid(conv_v)
        for index, part in enumerate(parts):
            queries[head, index] = query[part]
            key_rows[head, index] = key_low[part]
            values[head, index] = value[part]
    system, scores, inverse = {}, {}, {}
    for head, index in units:
        beta, _, _, _, causal = tables[head][index]
        key_blk = key_rows[head, index]
        system[head, index] = jnp.where(row > col, beta * mm(key_blk, key_blk, NT) * causal, 0.0)
        scores[head, index] = (mm(queries[head, index], key_blk, NT) * causal).astype(LOW)
    size = 1
    while size < CHUNK:
        own = (row // (2 * size) == col // (2 * size)) & (row // size != col // size)
        for unit in units:
            part = jnp.where(own, system[unit], 0.0)
            if size == 1:
                inverse[unit] = jnp.where(row == col, 1.0, 0.0) - part
            else:
                inverse_low = inverse[unit].astype(LOW)
                inverse[unit] = inverse[unit] - mm(mm(inverse_low, part), inverse_low)
        size *= 2
    gain = gain_ref[...]
    states = {head: jnp.zeros((head_dim, head_dim), FULL) for head in range(head_count)}
    for index, part in enumerate(parts):
        for head in range(head_count):
            unit = (head, index)
            cols = slice(head * head_dim, (head + 1) * head_dim)
            beta, start, tail, last, _ = tables[head][index]
            state = states[head]
            state_ref[head, index] = state.astype(LOW)
            inverse_low = inverse[unit].astype(LOW)
            inverse_ref[head, index] = inverse_low
            right = values[unit]
            if index:
                right = right - start * mm(key_rows[unit], state)
            fresh = mm(inverse_low, beta * right)
            fresh_low = fresh.astype(LOW)
            fresh_ref[part, cols] = fresh_low
            mixed = mm(scores[unit], fresh_low)
            if index:
                mixed = mixed + start * mm(queries[unit], state)
            mixed_ref[part, cols] = mixed
            if index + 1 < len(parts):
                grown = mm(key_rows[unit].astype(FULL) * tail, fresh_low, TN)
                states[head] = last * state + grown if index else grown
            gate = gate_ref[part, cols]
            scale = lax.rsqrt(jnp.mean(mixed * mixed, axis=-1, keepdims=True) + EPSILON)
            gated_ref[part, cols] = (mixed * scale * gain * (gate * sigmoid(gate))).astype(LOW)


def mixer_backward_body(
    grad_ref, query_ref, key_ref, value_ref, gate_ref, beta_ref, alpha_ref, taps_ref, dlog_ref,
    dbias_ref, gain_ref, mixed_ref, fresh_ref, inverse_ref, state_ref,
    dproj_ref, dbeta_ref, dalpha_ref, dtaps_ref, ddlog_ref, ddbias_ref, dgain_ref,
):
    rows, width = query_ref.shape
    head_dim = gain_ref.shape[1]
    head_count = width // head_dim
    parts = chunk_parts(rows)
    step = pl.program_id(0)
    first_head = step * head_count
    row, col = masks()
    decays, betas, shifted, tables = decay_tables(
        alpha_ref, beta_ref, dlog_ref, dbias_ref, first_head, head_count, parts
    )
    upper = jnp.where(row <= col, 1.0, 0.0)
    units = [(head, index) for head in range(head_count) for index in range(len(parts))]
    gain = gain_ref[...]
    root = 1.0 / math.sqrt(head_dim)
    all_cols = dproj_ref.shape[1] // 4

    def proj_cols(which, head):
        start = which * all_cols + (first_head + head) * head_dim
        return pl.ds(pl.multiple_of(start, head_dim), head_dim)

    @pl.when(step == 0)
    def _():
        dbeta_ref[...] = jnp.zeros_like(dbeta_ref)
        dalpha_ref[...] = jnp.zeros_like(dalpha_ref)
        ddlog_ref[...] = jnp.zeros_like(ddlog_ref)
        ddbias_ref[...] = jnp.zeros_like(ddbias_ref)
        dgain_ref[...] = jnp.zeros_like(dgain_ref)

    queries, key_rows, values, grads, acts, convs = {}, {}, {}, {}, {}, {}
    for head in range(head_count):
        cols = slice(head * head_dim, (head + 1) * head_dim)
        conv_q = conv_rows(query_ref[:, cols], taps_ref[0, :, cols])
        conv_k = conv_rows(key_ref[:, cols], taps_ref[1, :, cols])
        conv_v = conv_rows(value_ref[:, cols], taps_ref[2, :, cols])
        act_q = conv_q * sigmoid(conv_q)
        act_k = conv_k * sigmoid(conv_k)
        value = conv_v * sigmoid(conv_v)
        norm_q, norm_k = unit_inverse(act_q), unit_inverse(act_k)
        query, key_full = act_q * norm_q, act_k * norm_k
        convs[head] = (conv_q, conv_k, conv_v)
        acts[head] = (query, norm_q, key_full, norm_k)
        mixed = mixed_ref[:, cols]
        gate = gate_ref[:, cols]
        sig = sigmoid(gate)
        grad = grad_ref[:, cols]
        scale = lax.rsqrt(jnp.mean(mixed * mixed, axis=-1, keepdims=True) + EPSILON)
        normal = mixed * scale
        opened = gate * sig
        dgain_ref[...] += jnp.sum(grad * normal * opened, axis=0, keepdims=True)
        dproj_ref[:, proj_cols(3, head)] = (
            grad * normal * gain * (sig * (1.0 + gate * (1.0 - sig)))
        ).astype(LOW)
        grad_normal = grad * gain * opened
        grad_mixed = scale * (
            grad_normal - normal * jnp.mean(grad_normal * normal, axis=-1, keepdims=True)
        )
        for index, part in enumerate(parts):
            queries[head, index] = query[part] * root
            key_rows[head, index] = key_full[part]
            values[head, index] = value[part]
            grads[head, index] = grad_mixed[part]
    cross, scores, system, strict = {}, {}, {}, {}
    for unit in units:
        head, index = unit
        beta, _, _, _, causal = tables[head][index]
        cross[unit] = mm3(queries[unit], key_rows[unit], NT)
        scores[unit] = (cross[unit] * causal).astype(LOW)
        strict[unit] = jnp.where(row > col, beta * causal, 0.0)
        system[unit] = mm3(key_rows[unit], key_rows[unit], NT)
    grad_states = {head: None for head in range(head_count)}
    grad_q, grad_k, grad_v, gamma_grads = {}, {}, {}, {}
    grad_beta = {}
    for index in reversed(range(len(parts))):
        part = parts[index]
        for head in range(head_count):
            unit = (head, index)
            cols = slice(head * head_dim, (head + 1) * head_dim)
            beta, start, tail, last, causal = tables[head][index]
            query, key_full = queries[unit], key_rows[unit]
            query_low, key_low = query.astype(LOW), key_full.astype(LOW)
            grad = grads[unit]
            grad_low = grad.astype(LOW)
            fresh_low = fresh_ref[part, cols]
            fresh = fresh_low.astype(FULL)
            state = state_ref[head, index]
            grad_state = grad_states[head]
            grad_fresh = mm(scores[unit], grad_low, TN)
            if grad_state is not None:
                grad_state_low = grad_state.astype(LOW)
                grad_fresh = grad_fresh + mm(key_full * tail, grad_state_low)
            grad_right = mm(inverse_ref[head, index], grad_fresh, TN)
            grad_right_low = grad_right.astype(LOW)
            grad_cross = mm(grad_low, fresh_low, NT) * causal
            grad_system = -(mm(grad_right_low, fresh_low, NT) * strict[unit])
            turned = grad_cross * cross[unit] + grad_system * system[unit]
            gamma = row_sum(turned) - row_sum(turned.T)
            grad_cross_low = grad_cross.astype(LOW)
            grad_system_low = grad_system.astype(LOW)
            dquery = mm(grad_cross_low, key_low)
            dkey = (
                mm(grad_system_low, key_low)
                + mm(grad_system_low, key_low, TN)
                + mm(grad_cross_low, query_low, TN)
            )
            back = -beta * start * grad_right
            if index:
                back_low = back.astype(LOW)
                dquery = dquery + start * mm(grad_low, state, NT)
                dkey = dkey + mm(back_low, state, NT)
                gamma = gamma + row_sum(grad * start * mm(query_low, state))
                gamma = gamma + row_sum(back * mm(key_low, state))
            final = None
            if grad_state is not None:
                grad_tail = mm(fresh_low, grad_state_low, NT) * tail
                dkey = dkey + grad_tail
                tail_term = row_sum(grad_tail * key_full)
                gamma = gamma - tail_term
                final = jnp.sum(tail_term, axis=0, keepdims=True)
                if index:
                    final = final + last * jnp.sum(
                        row_sum(state.astype(FULL) * grad_state), axis=0, keepdims=True
                    )
                is_last = lax.broadcasted_iota(jnp.int32, gamma.shape, 0) == CHUNK - 1
                gamma = gamma + jnp.where(is_last, final, 0.0)
            gamma_grads[unit] = gamma
            grad_beta[unit] = (1.0 - beta) * row_sum(grad_right * fresh)
            grad_q[unit], grad_k[unit], grad_v[unit] = dquery, dkey, beta * grad_right
            if index:
                grown = mm(query * start, grad_low, TN) + mm(key_low, back_low, TN)
                if grad_state is not None:
                    grown = grown + last * grad_state
                grad_states[head] = grown
    lane = lax.broadcasted_iota(jnp.int32, (CHUNK, alpha_ref.shape[1]), 1)
    for index, part in enumerate(parts):
        gamma_cols = jnp.zeros(lane.shape, FULL)
        beta_cols = jnp.zeros(lane.shape, FULL)
        for head in range(head_count):
            gamma_cols = jnp.where(lane == first_head + head, gamma_grads[head, index], gamma_cols)
            beta_cols = jnp.where(lane == first_head + head, grad_beta[head, index], beta_cols)
        grad_decay = full_dot(upper, gamma_cols)
        grad_alpha = grad_decay * -jnp.exp(dlog_ref[...]) * sigmoid(shifted[part])
        dbeta_ref[part] += beta_cols
        dalpha_ref[part] += grad_alpha
        ddbias_ref[...] += jnp.sum(grad_alpha, axis=0, keepdims=True)
        ddlog_ref[...] += jnp.sum(grad_decay * decays[part], axis=0, keepdims=True)
    for head in range(head_count):
        cols = slice(head * head_dim, (head + 1) * head_dim)
        query, norm_q, key_full, norm_k = acts[head]
        dquery = jnp.concatenate([grad_q[head, index] for index in range(len(parts))], axis=0)
        dkey = jnp.concatenate([grad_k[head, index] for index in range(len(parts))], axis=0)
        dvalue = jnp.concatenate([grad_v[head, index] for index in range(len(parts))], axis=0)
        act_grads = (
            norm_q * root * (dquery - query * row_sum(query * dquery)),
            norm_k * (dkey - key_full * row_sum(key_full * dkey)),
            dvalue,
        )
        projected = (query_ref, key_ref, value_ref)
        for which in range(3):
            conv = convs[head][which]
            sig = sigmoid(conv)
            grad_conv = act_grads[which] * sig * (1.0 + conv * (1.0 - sig))
            grad_in, grad_taps = conv_back(
                grad_conv, projected[which][:, cols], taps_ref[which, :, cols]
            )
            dproj_ref[:, proj_cols(which, head)] = grad_in.astype(LOW)
            for tap, entry in enumerate(grad_taps):
                dtaps_ref[which, tap : tap + 1, cols] = entry


def mixer_specs(rows, heads, group, head_dim, taps_shape):
    width = group * head_dim
    wide = pl.BlockSpec((rows, width), lambda step: (0, step))
    narrow = pl.BlockSpec((rows, heads), lambda step: (0, 0))
    taps = pl.BlockSpec(taps_shape[:2] + (width,), lambda step: (0, 0, step))
    small = pl.BlockSpec((1, heads), lambda step: (0, 0))
    gain = pl.BlockSpec((1, head_dim), lambda step: (0, 0))
    chunks = rows // CHUNK
    square = pl.BlockSpec((group, chunks, CHUNK, CHUNK), lambda step: (step, 0, 0, 0))
    state = pl.BlockSpec((group, chunks, head_dim, head_dim), lambda step: (step, 0, 0, 0))
    return wide, narrow, taps, small, gain, square, state


def mixer_forward(projections, conv_taps, decay_log, decay_bias, norm_head):
    query, key_rows, value, gate, beta, alpha = projections
    rows, width = query.shape
    heads, head_dim = decay_log.shape[0], norm_head.shape[0]
    group = 2 if heads % 2 == 0 else 1
    chunks = rows // CHUNK
    wide, narrow, taps, small, gain, square, state = mixer_specs(
        rows, heads, group, head_dim, conv_taps.shape
    )
    return pl.pallas_call(
        mixer_forward_body,
        grid=(heads // group,),
        in_specs=[wide] * 4 + [narrow] * 2 + [taps, small, small, gain],
        out_specs=[wide, wide, wide, square, state],
        out_shape=[
            jax.ShapeDtypeStruct((rows, width), LOW),
            jax.ShapeDtypeStruct((rows, width), FULL),
            jax.ShapeDtypeStruct((rows, width), LOW),
            jax.ShapeDtypeStruct((heads, chunks, CHUNK, CHUNK), LOW),
            jax.ShapeDtypeStruct((heads, chunks, head_dim, head_dim), LOW),
        ],
        compiler_params=pltpu.CompilerParams(
            vmem_limit_bytes=48 * 1024 * 1024, dimension_semantics=("arbitrary",)
        ),
        name="mixer_forward",
    )(
        query, key_rows, value, gate, beta, alpha, conv_taps,
        decay_log.reshape(1, heads), decay_bias.reshape(1, heads), norm_head.reshape(1, head_dim),
    )


def mixer_backward(grad, projections, conv_taps, decay_log, decay_bias, norm_head, kept):
    query, key_rows, value, gate, beta, alpha = projections
    mixed, fresh, inverse, states = kept
    rows, width = query.shape
    heads, head_dim = decay_log.shape[0], norm_head.shape[0]
    group = 2 if heads % 2 == 0 else 1
    wide, narrow, taps, small, gain, square, state = mixer_specs(
        rows, heads, group, head_dim, conv_taps.shape
    )
    return pl.pallas_call(
        mixer_backward_body,
        grid=(heads // group,),
        in_specs=[wide] * 5
        + [narrow] * 2
        + [taps, small, small, gain, wide, wide, square, state],
        out_specs=[pl.BlockSpec((rows, 4 * width), lambda step: (0, 0))]
        + [narrow] * 2
        + [taps, small, small, gain],
        out_shape=[jax.ShapeDtypeStruct((rows, 4 * width), LOW)]
        + [jax.ShapeDtypeStruct((rows, heads), FULL)] * 2
        + [
            jax.ShapeDtypeStruct(conv_taps.shape, FULL),
            jax.ShapeDtypeStruct((1, heads), FULL),
            jax.ShapeDtypeStruct((1, heads), FULL),
            jax.ShapeDtypeStruct((1, head_dim), FULL),
        ],
        compiler_params=pltpu.CompilerParams(
            vmem_limit_bytes=48 * 1024 * 1024, dimension_semantics=("arbitrary",)
        ),
        name="mixer_backward",
    )(
        grad, query, key_rows, value, gate, beta, alpha, conv_taps,
        decay_log.reshape(1, heads), decay_bias.reshape(1, heads), norm_head.reshape(1, head_dim),
        mixed, fresh, inverse, states,
    )


def rms_scale(vector, gain):
    return vector * lax.rsqrt(jnp.mean(vector * vector, axis=-1, keepdims=True) + EPSILON) * gain


def rms_back(grad_norm, vector, gain):
    inverse = lax.rsqrt(jnp.mean(vector * vector, axis=-1, keepdims=True) + EPSILON)
    normal = vector * inverse
    scaled = grad_norm * gain
    return inverse * (scaled - normal * jnp.mean(scaled * normal, axis=-1, keepdims=True))


def codes(parts):
    masks = []
    while 1 << len(masks) < parts:
        masks.append((2 << len(masks)) - 1)
    order = []
    for code in range(parts):
        place = 0
        for index, mask in enumerate(masks):
            if code >> (len(masks) - 1 - index) & 1:
                place ^= mask
        order.append(place)
    return masks, order


def own_code():
    order = codes(lax.axis_size("head"))[1]
    place = lax.axis_index("head")
    return sum(jnp.where(place == at, code, 0) for code, at in enumerate(order))


def scatter_steps(partial_sum):
    parts = lax.axis_size("head")
    code = own_code()
    for mask in codes(parts)[0]:
        half = partial_sum.shape[0] // 2
        parts //= 2
        bit = lax.rem(code // parts, 2)
        payload = lax.dynamic_slice_in_dim(partial_sum, (1 - bit) * half, half, 0)
        kept = lax.dynamic_slice_in_dim(partial_sum, bit * half, half, 0)
        pairs = [(at, at ^ mask) for at in range(lax.axis_size("head"))]
        (other,) = yield [(payload.astype(LOW), "head", pairs)]
        partial_sum = kept.astype(FULL) + other.astype(FULL)
    return partial_sum


def gather_steps(own, buffer=None, micro=0):
    parts = lax.axis_size("head")
    code = own_code()
    step = 1
    for mask in codes(parts)[0][::-1]:
        (other,) = yield [(own, "head", [(at, at ^ mask) for at in range(parts)])]
        bit = lax.rem(code // step, 2)
        size = own.shape[0]
        step *= 2
        if buffer is not None and step == parts:
            for piece, index in ((own, bit), (other, 1 - bit)):
                buffer[0] = lax.dynamic_update_slice(
                    buffer[0], piece[None], (micro, index * size, 0)
                )
            return buffer
        shape = list(own.shape)
        shape[0] *= 2
        joined = jnp.zeros(shape, own.dtype)
        joined = lax.dynamic_update_slice_in_dim(joined, own, bit * size, 0)
        own = lax.dynamic_update_slice_in_dim(joined, other, (1 - bit) * size, 0)
    return own


OUTER, INNER, BACK = [(0, 1), (3, 2)], [(1, 2), (2, 1)], [(1, 0), (2, 3)]


def hub_scatter_steps(partial_sum):
    half = partial_sum.shape[0] // 2
    bit = lax.axis_index("head") // 2
    near = lax.dynamic_slice_in_dim(partial_sum, bit * half, half, 0)
    far = lax.dynamic_slice_in_dim(partial_sum, (1 - bit) * half, half, 0)
    (first,) = yield [(far, "head", OUTER)]
    passed = (far.astype(FULL) + first.astype(FULL)).astype(LOW)
    second, last = yield [(passed, "head", INNER), (near, "head", OUTER)]
    return near.astype(FULL) + second.astype(FULL) + last.astype(FULL)


def hub_gather_steps(own, buffer=None, micro=0):
    half, width = own.shape
    place = lax.axis_index("head")
    bit = place // 2
    middle = (place == 1) | (place == 2)
    other, near = yield [(own, "head", INNER), (own, "head", BACK)]
    (far,) = yield [(other, "head", BACK)]
    pieces = (jnp.where(middle, own, near), bit), (jnp.where(middle, other, far), 1 - bit)
    if buffer is None:
        whole = jnp.zeros((2 * half, width), own.dtype)
        for piece, index in pieces:
            whole = lax.dynamic_update_slice_in_dim(whole, piece, index * half, 0)
        return whole
    for piece, index in pieces:
        buffer[0] = lax.dynamic_update_slice(buffer[0], piece[None], (micro, index * half, 0))
    return buffer


def batch_scatter_steps(value):
    size = lax.axis_size("batch")
    place = lax.axis_index("batch")
    while size > 1:
        size //= 2
        half = value.shape[0] // 2
        bit = lax.rem(place // size, 2)
        payload = lax.dynamic_slice_in_dim(value, (1 - bit) * half, half, 0)
        kept = lax.dynamic_slice_in_dim(value, bit * half, half, 0)
        (other,) = yield [
            (payload.astype(LOW), "batch", [(at, at ^ size) for at in range(lax.axis_size("batch"))])
        ]
        value = kept.astype(FULL) + other.astype(FULL)
    return value


def butterfly_steps(local, wide):
    for axis in ("batch", "head"):
        size = lax.axis_size(axis)
        bit = 1
        while bit < size:
            value = jnp.concatenate([local, wide], axis=0) if axis == "batch" else wide
            (other,) = yield [(value, axis, [(at, at ^ bit) for at in range(size)])]
            value = value + other
            if axis == "batch":
                local, wide = value[: local.shape[0]], value[local.shape[0] :]
            else:
                wide = value
            bit *= 2
    return local, wide


LAG = 2


class Flow:
    def __init__(self, steps, lag=0):
        self.steps = steps
        self.lag = lag
        self.fresh = True
        self.result = None
        self.advance(None)

    def advance(self, received):
        self.fresh = True
        try:
            self.pending = self.steps.send(received)
        except StopIteration as stop:
            self.pending = None
            self.result = stop.value


class Clock:
    def __init__(self):
        self.flows = []
        self.due = []

    def join(self, steps, lag=0):
        flow = Flow(steps, lag)
        self.flows.append(flow)
        return flow

    def step(self, work=None):
        flows = [flow for flow in self.flows if flow.pending is not None]
        for flow in flows:
            self.due.extend([flow.lag, request[0]] for request in flow.pending)
        token = ()
        if work is not None:
            ahead = [value for lag, value in self.due if lag <= 0]
            token = work(lambda value: after(value, *ahead) if ahead else value)
            token = tuple(token) if isinstance(token, (tuple, list)) else (token,)
            self.due = [[lag - 1, value] for lag, value in self.due if lag > 0]
        for flow in flows:
            received = [lax.ppermute(*request) for request in flow.pending]
            if token:
                received = lax.optimization_barrier(tuple(received) + token)[: len(received)]
            flow.advance(received)
            if flow.pending is None:
                self.due.extend([flow.lag, value] for value in received)
        self.flows = [flow for flow in flows if flow.pending is not None]

    def until(self, flow):
        while flow.result is None:
            self.step()
        return flow.result


def packed(entries):
    flat = jnp.concatenate([entry.reshape(-1) for entry in entries])
    pad = -flat.shape[0] % 1024
    return jnp.pad(flat, (0, pad)).reshape(-1, 128)


def unpacked(matrix, entries):
    flat = matrix.reshape(-1)
    outs, start = [], 0
    for entry in entries:
        outs.append(flat[start : start + entry.size].reshape(entry.shape))
        start += entry.size
    return outs


def after(value, *others):
    return lax.optimization_barrier((value,) + others)[0]


def per_device(
    tokens, cotangent, lengths, norm_in, w_query, w_key, w_value, w_gate, w_beta, w_alpha,
    conv_taps, decay_log, decay_bias, norm_head, w_out, norm_mid, w_up_gate, w_up, w_down,
):
    micro_count, seq_len, model_dim = tokens.shape
    head_parts = lax.axis_size("head")
    batch_parts = lax.axis_size("batch")
    hub = False
    place = lax.axis_index("head")
    if hub:
        own_len = seq_len // 2
        first_row = place // 2 * own_len
        counts = jnp.where((place == 1) | (place == 2), 1.0, 0.0)
        scatter, gather = hub_scatter_steps, hub_gather_steps
    else:
        own_len = seq_len // head_parts
        first_row = own_code() * own_len
        counts = 1.0
        scatter, gather = scatter_steps, gather_steps
    positions = lax.broadcasted_iota(jnp.int32, (seq_len, 1), 0)
    in_weights = (w_query, w_key, w_value, w_gate)
    hidden_width = w_up.shape[1]
    head_width = w_query.shape[1]

    def own_of(value):
        return lax.dynamic_slice_in_dim(value, first_row, own_len, 0)

    class Micro:
        def __init__(self, micro):
            self.micro = micro
            keep = (positions < lengths[micro, 0]).astype(LOW)
            self.rows = own_of(tokens[micro]).astype(FULL)
            self.grad_rows = own_of(cotangent[micro]).astype(FULL)
            self.keep_own = own_of(keep).astype(FULL)
            self.down_grad = keep * cotangent[micro]


        def project(self, tie):
            rows = tie(tokens[self.micro]).astype(FULL)
            self.normed = rms_scale(rows, norm_in).astype(LOW)
            self.projections = tuple(
                mm(self.normed, weight) for weight in in_weights + (w_beta, w_alpha)
            )
            return self.projections

        def mix(self, tie):
            query, *others = self.projections
            self.projections = (tie(query), *others)
            self.gated, *self.kept = mixer_forward(
                self.projections, conv_taps, decay_log, decay_bias, norm_head
            )
            return self.gated

        def project_out(self, tie):
            self.out_part = mm(tie(self.gated), w_out).astype(LOW)
            return self.out_part

        def after_mixer(self, out_sum):
            self.middle = self.rows + self.keep_own * out_sum
            return join(gather(rms_scale(self.middle, norm_mid).astype(LOW)))

        def up(self, tie):
            mid = tie(self.mid)
            self.gate_act, self.up_act = mm(mid, w_up_gate), mm(mid, w_up)
            return self.gate_act, self.up_act

        def activate(self, tie):
            gate_act, up_act = tie(self.gate_act), self.up_act
            grad_hidden = mm(self.down_grad, w_down, NT)
            sig = jax.nn.sigmoid(gate_act)
            opened = gate_act * sig
            self.hidden = (opened * up_act).astype(LOW)
            self.grad_gate = (
                grad_hidden * up_act * sig * (1.0 + gate_act * (1.0 - sig))
            ).astype(LOW)
            self.grad_up = (grad_hidden * opened).astype(LOW)
            return self.hidden, self.grad_gate, self.grad_up

        def up_back(self, tie):
            self.mid_part = (
                mm(tie(self.grad_gate), w_up_gate, NT) + mm(self.grad_up, w_up, NT)
            ).astype(LOW)
            return self.mid_part

        def down(self, tie):
            self.down_part = mm(tie(self.hidden), w_down).astype(LOW)
            return self.down_part

        def after_down(self, down_sum):
            own = (self.middle + self.keep_own * down_sum).astype(LOW)
            return join(gather(own, out_buffer, self.micro), 3)

        def after_up_back(self, mid_sum):
            self.gain_mid = counts * jnp.sum(rms_scale(self.middle, 1.0) * mid_sum, axis=0)
            self.grad_middle = self.grad_rows + rms_back(mid_sum, self.middle, norm_mid)
            return join(gather((self.keep_own * self.grad_middle).astype(LOW)))

        def mix_back(self, tie):
            grad_gated = mm(tie(self.attn), w_out, NT)
            self.grads, grad_beta, grad_alpha, *self.small = mixer_backward(
                grad_gated, self.projections, conv_taps, decay_log, decay_bias,
                norm_head, self.kept,
            )
            self.beta, self.alpha = grad_beta.astype(LOW), grad_alpha.astype(LOW)
            return self.grads

        def project_back(self, tie):
            grads = tie(self.grads)
            in_part = mm(self.beta, w_beta, NT) + mm(self.alpha, w_alpha, NT)
            for index, weight in enumerate(in_weights):
                in_part = in_part + mm(
                    grads[:, index * head_width : (index + 1) * head_width], weight, NT
                )
            self.in_part = in_part.astype(LOW)
            rows = tokens[self.micro].astype(FULL)
            self.gain_in = jnp.sum(rms_scale(rows, 1.0) * in_part, axis=0)
            return self.in_part, self.gain_in

        def after_project_back(self, in_sum):
            own = (self.grad_middle + rms_back(in_sum, self.rows, norm_in)).astype(LOW)
            return join(gather(own, grad_buffer, self.micro), 3)

    clock = Clock()
    join, step, until = clock.join, clock.step, clock.until
    out_buffer, grad_buffer = [jnp.zeros_like(tokens)], [jnp.zeros_like(tokens)]
    one, two = Micro(0), Micro(1)
    held = (one, two)

    def both(*names):
        return jnp.concatenate(
            [jnp.concatenate([getattr(h, name) for name in names], axis=1) for h in held], axis=0
        )

    def shared(product):
        return lax.psum_scatter(product, "batch", scatter_dimension=0, tiled=True)

    def together(*works):
        def run(tie):
            token = ()
            for work in works:
                value = work(tie)
                token += tuple(value) if isinstance(value, (tuple, list)) else (value,)
            return token

        return run

    product = {}

    def ups_product(tie):
        product["ups"] = mm(tie(both("mid")), both("grad_gate", "grad_up"), TN).astype(LOW)
        return product["ups"]

    def downs_product(tie):
        downs = mm(tie(both("down_grad")), both("hidden"), TN).astype(LOW)
        product["ff"] = jnp.concatenate([product["ups"], downs], axis=1)
        return product["ff"]

    def out_product(tie):
        product["out"] = mm(tie(both("attn")), both("gated"), TN).astype(LOW)
        return product["out"]

    def in_product(tie):
        normed = after(tie(both("normed")), share_ff)
        product["in"] = mm(normed, both("grads"), TN).astype(LOW)
        product["tiny"] = mm(both("beta", "alpha"), normed, TN)
        return product["in"], product["tiny"]

    def free(value):
        return value

    one.project(free), one.mix(free), one.project_out(free)
    sum_one = join(scatter(one.out_part))
    step(lambda tie: two.project(lambda value: after(tie(value), one.out_part)))
    step(two.mix)
    until(sum_one)
    mid_one = one.after_mixer(sum_one.result)
    two.project_out(free)
    sum_two = join(scatter(two.out_part))
    one.mid = until(mid_one)
    mid_two = two.after_mixer(until(sum_two))
    step(one.up)
    step(together(one.activate, one.up_back))
    sum_one = join(scatter(one.mid_part))
    two.mid = until(mid_two)
    step(together(one.down, two.up))
    down_one = join(scatter(one.down_part), LAG)
    step(together(two.activate, two.up_back))
    attn_one = one.after_up_back(until(sum_one))
    sum_two = join(scatter(two.mid_part))
    step(ups_product)
    step(together(downs_product, two.down))
    share_ff = shared(product["ff"])
    out_one = one.after_down(until(down_one))
    one.attn = until(attn_one)
    attn_two = two.after_up_back(until(sum_two))
    down_two = join(scatter(two.down_part), LAG)
    step(one.mix_back)
    step(one.project_back)
    sum_one = join(scatter(one.in_part), LAG)
    two.attn = until(attn_two)
    step(
        together(
            out_product, lambda tie: two.mix_back(lambda value: after(tie(value), one.in_part))
        )
    )
    out_flow = join(batch_scatter_steps(product["out"]), 4)
    step(in_product)
    share_in = shared(product["in"])
    step(two.project_back)
    sum_two = join(scatter(two.in_part))
    small = [a + b for a, b in zip(one.small, two.small)]
    local = (product["tiny"], small[0], small[1][0], small[2][0])
    wide = (one.gain_in + two.gain_in, small[3][0], one.gain_mid + two.gain_mid)
    small_flow = join(butterfly_steps(packed(local), packed(wide)))
    out_two = two.after_down(until(down_two))
    grad_one = one.after_project_back(until(sum_one))
    grad_two = two.after_project_back(until(sum_two))
    while clock.flows:
        step()
    tiny, grad_taps, grad_dlog, grad_dbias = unpacked(small_flow.result[0], local)
    gains = unpacked(small_flow.result[1], wide)
    width = model_dim // batch_parts
    tiny = lax.dynamic_slice_in_dim(tiny, lax.axis_index("batch") * width, width, 1).T
    count = w_beta.shape[1]

    def pieces(matrix, *widths):
        outs, start = [], 0
        for extent in widths:
            outs.append(matrix[:, start : start + extent].astype(FULL))
            start += extent
        return outs

    share_in = pieces(share_in, *([head_width] * 4))
    share_gate, share_up, share_down = pieces(share_ff, *([hidden_width] * 3))
    return (
        out_buffer[0],
        grad_buffer[0],
        gains[0], *share_in, tiny[:, :count], tiny[:, count:],
        grad_taps, grad_dlog, grad_dbias, gains[1],
        out_flow.result.T, gains[2], share_gate, share_up, share_down.T,
    )


def solution(mesh):
    tokens, column, row = P(None, "batch", None), P(None, "head"), P("head", None)
    placed = (
        tokens, tokens, P(None, "batch"), P(), column, column, column, column, column, column,
        P(None, None, "head"), P("head"), P("head"), P(), row, P(), column, column, row,
    )
    block, turned = P("batch", "head"), P("head", "batch")
    return jax.shard_map(
        per_device,
        mesh=mesh,
        in_specs=placed,
        out_specs=(
            tokens, tokens, P(), block, block, block, block, block, block,
            P(None, None, "head"), P("head"), P("head"), P(), turned, P(), block, block, turned,
        ),
        check_vma=False,
    )
```
